32 devices in a mesh: req: 4 (over x, core), mlp: 8 (over z, y).
Axes of the slice: x: 2, y: 2, z: 4, core: 2. Of those that a mesh axis runs over, the one named last changes fastest.
Arguments:
- queries: bfloat16 [1024, 4096], P(('req', 'mlp')), may hold values from -80 to 80
- keys: bfloat16 [1024, 4096], P(('req', 'mlp')), may hold values from -4 to 4
- values: bfloat16 [1024, 4096], P(('req', 'mlp')), may hold values from -6 to 6
- block_hidden_input: bfloat16 [1024, 5120], P(('req', 'mlp')), may hold values from -6 to 6
- attention_out_weight: bfloat16 [4096, 5120], P('mlp'), may hold values from -0.09375 to 0.09375
- feedfwd_in_weight: bfloat16 [5120, 13824], P(None, 'mlp'), may hold values from -0.078125 to 0.078125
- feedfwd_out_weight: bfloat16 [13824, 5120], P('mlp'), may hold values from -0.0546875 to 0.0546875
- norm_gain_vector: float32 [5120], replicated, may hold values from 0.5 to 1.5
- norm_bias_vector: float32 [5120], replicated, may hold values from -3 to 3
- adapter_down_factors: bfloat16 [64, 5120, 16], P('req', 'mlp'), may hold values from -0.078125 to 0.078125
- adapter_up_factors: bfloat16 [64, 16, 13824], P('req', None, 'mlp'), may hold values from -0.75 to 0.75
- paged_key_cache: bfloat16 [12, 128, 4096], P('req', None, 'mlp'), may hold values from -6 to 6
- paged_value_cache: bfloat16 [12, 128, 4096], P('req', None, 'mlp'), may hold values from -6 to 6
- request_prompt_length: int32 [4, 16], P('req'), may hold values from 1 to 128, 256 in all within a row
- group_page_lookup: int32 [4, 2], P('req'), may hold values from 0 to 2, as said below
- adapter_per_request: int32 [4, 16], P('req'), may hold values from 0 to 63
- adapter_bank_slot: int32 [64], replicated, may hold values from 0 to 63, each once
Outputs:
- block_out: bfloat16 [1024, 5120], P(('req', 'mlp'))
- key_pages_out: bfloat16 [12, 128, 4096], P('req', None, 'mlp')
- value_pages_out: bfloat16 [12, 128, 4096], P('req', None, 'mlp')
The draws below stay inside these ranges and needn't reach their ends.
Inputs may be any that keep to these rules, and one draw needn't show every extreme that they name: `group_page_lookup`: the 2 entries of a row are different pages of the group's 3. `request_prompt_length`: each row sums to 256; its longest request holds exactly half of that.
All inputs are finite; a program needn't handle non-finite values.
Results may differ from the reference program's by a relative error of at most 0.014.
Values may be sent and summed in bfloat16 or wider, within the bound.
No kernel may reach another device: no remote copies, remote signals or barrier semaphores. Data moves between devices by JAX's collectives and lax.ppermute only.
A program may use at most 128 MiB of HBM per device.

```python
import math
import jax
import jax.numpy as jnp
import numpy as np
from jax import lax

MODEL_WIDTH = 5120
HEADS = 32
HS = 128
FEEDFWD_UNITS = 13824
ADAPTER_RANK = 16
ADAPTER_COUNT = 64
REQS = 16
PAGE = 128
TOK_DEV = 32
TOK_G = 256
TOKENS = 1024
BLOCKS = 2
PAGES = 3
N_REQ = 4
N_MLP = 8


def drawn_pair(key):
    head_width = HEADS * HS
    queries = jnp.clip(jax.random.normal(jax.random.fold_in(key, 11), (TOKENS, head_width), jnp.float32), -4.0, 4.0)
    keys = jnp.clip(jax.random.normal(jax.random.fold_in(key, 12), (TOKENS, head_width), jnp.float32), -4.0, 4.0)
    return (queries, keys)


def draw_queries(key, part):
    return drawn_pair(key)[0].astype(jnp.bfloat16)


def draw_keys(key, part):
    return drawn_pair(key)[1].astype(jnp.bfloat16)


def draw_group_page_lookup(key, part):

    def one_group(group_number):
        chosen = jax.random.permutation(jax.random.fold_in(key, group_number), PAGES)[:BLOCKS]
        holds_last = jnp.any(chosen == PAGES - 1)
        return chosen.at[0].set(jnp.where(holds_last, chosen[0], PAGES - 1))
    return jax.vmap(one_group)(jnp.arange(N_REQ)).astype(jnp.int32)


def place_ends(entries, rng, low, high):
    longest = entries.shape.index(max(entries.shape))
    spots = []
    for shift in (0, 1):
        where = [jax.random.randint(jax.random.fold_in(rng, axis), (), 0, length) for axis, length in enumerate(entries.shape)]
        where[longest] = (where[longest] + shift) % entries.shape[longest]
        spots.append(tuple(where))
    return entries.at[spots[0]].set(low).at[spots[1]].set(high)


def block_levels(own_key, dims, cuts, smallest, largest):
    factor_of, own = 1.0, jax.random.fold_in(own_key, 6)
    for dim, blocks in cuts:
        heights = jnp.exp(jax.random.uniform(jax.random.fold_in(own, dim), (blocks,), jnp.float32, smallest / len(cuts), largest / len(cuts)))
        factor_of = factor_of * jnp.repeat(heights, dims[dim] // blocks).reshape([-1 if axis == dim else 1 for axis in range(len(dims))])
    return factor_of


def rank_table(number_of, skew):
    loads = [(1 << 20) // math.isqrt(rank ** skew) + 1 for rank in range(1, number_of + 1)]
    scale = 1 + sum(loads) // (1 << 30)
    return np.cumsum(np.array([max(1, weight // scale) for weight in loads]))


def ranked_ids(rng, extent, number_of, lean):
    grid = rank_table(number_of, lean)
    ticket = jax.random.randint(jax.random.fold_in(rng, 1), extent, 0, int(grid[number_of - 1]))
    rank = jnp.searchsorted(jnp.asarray(grid, jnp.int32), ticket, side="right")
    return jax.random.permutation(jax.random.fold_in(rng, 2), number_of)[rank].astype(jnp.int32)


def length_profile(count, total, reach, skew):
    portions = [(1 << 20) // math.isqrt(rank ** skew) + 1 for rank in range(2, count + 1)]
    spare, counts = total - reach - (count - 1), [1] * (count - 1)
    while spare > 0:
        free = [i for i in range(count - 1) if counts[i] < reach]
        pool, left = sum([portions[i] for i in free]), spare
        for i in free:
            more = min(reach - counts[i], max(1, left * portions[i] // pool), spare)
            counts[i] = counts[i] + more
            spare = spare - more
    return np.array([reach] + counts)


def ragged(stream_key, count, total, bound, skew):
    if count == 2:
        one = jax.random.randint(stream_key, (), max(1, total - bound), min(bound, total - 1) + 1)
        return jnp.stack([one, total - one])
    sizes = jnp.asarray(length_profile(count, total, bound, skew), jnp.int32)
    twos = (count - 1) // 2
    source_of, sink = sizes[1:1 + 2 * twos:2], sizes[2:2 + 2 * twos:2]
    room = jnp.minimum(source_of - 1, bound - sink)
    passed = jax.random.randint(jax.random.fold_in(stream_key, 1), (twos,), 0, 1 << 20) % (room + 1)
    sizes = sizes.at[1:1 + 2 * twos:2].set(source_of - passed).at[2:2 + 2 * twos:2].set(sink + passed)
    return sizes[jax.random.permutation(jax.random.fold_in(stream_key, 2), count)]


def bell_draw(key, dims, deviation, bound, shards=(), held_as=jnp.bfloat16):
    factor_of = block_levels(key, dims, shards, -0.22, 0.18) if shards else 1.0
    values = jax.random.normal(key, dims, jnp.float32) * deviation * factor_of
    return jnp.minimum(jnp.maximum(values, -bound), bound).astype(held_as)


def setup_inputs(seed: int = 0) -> dict:
    seeds = jax.random.split(jax.random.key(seed), 18)
    queries = draw_queries(jax.random.fold_in(seeds[17], 71), 0)
    keys = draw_keys(jax.random.fold_in(seeds[17], 71), 0)
    values = bell_draw(seeds[2], (TOKENS, HEADS * HS), 1.0, 6.0, ((0, 32),))
    block_hidden_input = bell_draw(seeds[3], (TOKENS, MODEL_WIDTH), 1.0, 6.0, ((0, 32),))
    attention_out_weight = bell_draw(seeds[4], (HEADS * HS, MODEL_WIDTH), (HEADS * HS) ** -0.5, 0.09375, ((0, 8),))
    feedfwd_in_weight = bell_draw(seeds[5], (MODEL_WIDTH, FEEDFWD_UNITS), MODEL_WIDTH ** -0.5, 0.078125, ((1, 8),))
    feedfwd_out_weight = bell_draw(seeds[6], (FEEDFWD_UNITS, MODEL_WIDTH), FEEDFWD_UNITS ** -0.5, 0.0546875, ((0, 8),))
    norm_gain_vector = jnp.clip(1.0 + 0.1 * jax.random.normal(seeds[7], (MODEL_WIDTH,), jnp.float32), 0.5, 1.5)
    norm_bias_vector = bell_draw(seeds[8], (MODEL_WIDTH,), 0.5, 3.0, (), jnp.float32)
    adapter_down_factors = bell_draw(seeds[9], (ADAPTER_COUNT, MODEL_WIDTH, ADAPTER_RANK), MODEL_WIDTH ** -0.5, 0.078125, ((0, 4), (1, 8)))
    adapter_up_factors = bell_draw(seeds[10], (ADAPTER_COUNT, ADAPTER_RANK, FEEDFWD_UNITS), (4 * ADAPTER_RANK) ** -0.5, 0.75, ((0, 4), (2, 8)))
    paged_key_cache = bell_draw(seeds[11], (N_REQ * PAGES, PAGE, HEADS * HS), 1.0, 6.0, ((0, 4), (2, 8)))
    paged_value_cache = bell_draw(seeds[12], (N_REQ * PAGES, PAGE, HEADS * HS), 1.0, 6.0, ((0, 4), (2, 8)))
    request_prompt_length = jax.vmap(lambda own: ragged(own, REQS, TOK_G, TOK_G // 2, 2))(jax.random.split(seeds[13], N_REQ)).reshape((N_REQ, REQS)).astype(jnp.int32)
    group_page_lookup = draw_group_page_lookup(jax.random.fold_in(seeds[17], 71), 0)
    adapter_per_request = place_ends(ranked_ids(seeds[15], (N_REQ, REQS), ADAPTER_COUNT, 2), jax.random.fold_in(seeds[15], 3), 0, ADAPTER_COUNT - 1).astype(jnp.int32)
    adapter_bank_slot = jax.random.permutation(seeds[16], ADAPTER_COUNT).astype(jnp.int32)
    return {"queries": queries, "keys": keys, "values": values, "block_hidden_input": block_hidden_input, "attention_out_weight": attention_out_weight, "feedfwd_in_weight": feedfwd_in_weight, "feedfwd_out_weight": feedfwd_out_weight, "norm_gain_vector": norm_gain_vector, "norm_bias_vector": norm_bias_vector, "adapter_down_factors": adapter_down_factors, "adapter_up_factors": adapter_up_factors, "paged_key_cache": paged_key_cache, "paged_value_cache": paged_value_cache, "request_prompt_length": request_prompt_length, "group_page_lookup": group_page_lookup, "adapter_per_request": adapter_per_request, "adapter_bank_slot": adapter_bank_slot}


EPS = 1e-06

def modulate(residual, norm_gain_vector, norm_bias_vector):
    row_mean = lax.optimization_barrier(jnp.mean(residual, axis=-1, keepdims=True))
    centered = residual - row_mean
    row_var = lax.optimization_barrier(jnp.mean(centered * centered, axis=-1, keepdims=True))
    return (centered * lax.rsqrt(row_var + EPS) * norm_gain_vector + norm_bias_vector).astype(jnp.bfloat16)

def softmax_rows(scores, allowed):
    masked = jnp.where(allowed, scores, -1e+30)
    row_peak = lax.optimization_barrier(jnp.max(masked, axis=-1, keepdims=True))
    exponent = jnp.exp(masked - row_peak)
    return (exponent / lax.optimization_barrier(jnp.sum(exponent, axis=-1, keepdims=True))).astype(jnp.bfloat16)

def block_rounded_product(left, right, blocks):
    inner = left.shape[1] // blocks
    result = jnp.zeros((left.shape[0], right.shape[1]), jnp.float32)
    for index_block in range(blocks):
        block_sum = jnp.dot(left[:, index_block * inner:(index_block + 1) * inner], right[index_block * inner:(index_block + 1) * inner], preferred_element_type=jnp.float32)
        rounded = lax.optimization_barrier(block_sum.astype(jnp.bfloat16))
        result = result + rounded.astype(jnp.float32)
    return result

def reference(queries, keys, values, block_hidden_input, attention_out_weight, feedfwd_in_weight, feedfwd_out_weight, norm_gain_vector, norm_bias_vector, adapter_down_factors, adapter_up_factors, paged_key_cache, paged_value_cache, request_prompt_length, group_page_lookup, adapter_per_request, adapter_bank_slot):
    group_rows = TOK_DEV * N_MLP
    head_width = HEADS * HS
    positions = jnp.arange(group_rows, dtype=jnp.int32)
    request_ends = jnp.cumsum(request_prompt_length, axis=1).astype(jnp.int32)
    segments = lax.optimization_barrier(jnp.sum((positions[None, :, None] >= request_ends[:, None, :]).astype(jnp.int32), axis=2)).astype(jnp.int32)
    score_scale = HS ** (-0.5)

    def attend(group_data):
        query_group, key_group, value_group, group_segment = group_data
        query_heads = query_group.reshape(group_rows, HEADS, HS).astype(jnp.float32)
        key_heads = key_group.reshape(group_rows, HEADS, HS).astype(jnp.float32)
        value_heads = value_group.reshape(group_rows, HEADS, HS).astype(jnp.float32)
        scores = jnp.einsum('qhd,khd->hqk', query_heads, key_heads) * score_scale
        allowed = (group_segment[:, None] == group_segment[None, :]) & (positions[None, :] <= positions[:, None])
        weights = softmax_rows(scores, allowed[None]).astype(jnp.float32)
        mixed = jnp.einsum('hqk,khd->qhd', weights, value_heads)
        return mixed.astype(jnp.bfloat16).reshape(group_rows, head_width)
    attended = lax.map(attend, (queries.reshape(N_REQ, group_rows, head_width), keys.reshape(N_REQ, group_rows, head_width), values.reshape(N_REQ, group_rows, head_width), segments)).reshape(TOKENS, head_width)
    group_index = jnp.arange(N_REQ, dtype=jnp.int32)[:, None]
    key_pages_out = paged_key_cache.reshape(N_REQ, PAGES, PAGE, head_width).at[group_index, group_page_lookup].set(keys.reshape(N_REQ, BLOCKS, PAGE, head_width)).reshape(N_REQ * PAGES, PAGE, head_width)
    value_pages_out = paged_value_cache.reshape(N_REQ, PAGES, PAGE, head_width).at[group_index, group_page_lookup].set(values.reshape(N_REQ, BLOCKS, PAGE, head_width)).reshape(N_REQ * PAGES, PAGE, head_width)
    residual = block_hidden_input.astype(jnp.float32) + block_rounded_product(attended, attention_out_weight, N_MLP)
    normed = modulate(residual, norm_gain_vector, norm_bias_vector)
    slots = adapter_bank_slot[adapter_per_request]

    def adapt(group_data):
        normed_group, group_segment, group_bank_slots = group_data
        down_factor_chosen = adapter_down_factors[group_bank_slots].astype(jnp.float32)
        up_factor_chosen = adapter_up_factors[group_bank_slots].astype(jnp.float32)
        chosen = (group_segment[:, None] == jnp.arange(REQS, dtype=jnp.int32)[None, :]).astype(jnp.float32)
        every_rank = jnp.einsum('td,rdk->trk', normed_group.astype(jnp.float32), down_factor_chosen)
        lowrank = lax.optimization_barrier(lax.optimization_barrier(jnp.sum(every_rank * chosen[:, :, None], axis=1)).astype(jnp.bfloat16))
        spread = chosen[:, :, None] * lowrank.astype(jnp.float32)[:, None, :]
        preact = jnp.dot(normed_group, feedfwd_in_weight, preferred_element_type=jnp.float32) + jnp.einsum('trk,rkf->tf', spread, up_factor_chosen)
        return jax.nn.gelu(preact, approximate=True).astype(jnp.bfloat16)
    activated = lax.map(adapt, (normed.reshape(N_REQ, group_rows, MODEL_WIDTH), segments, slots)).reshape(TOKENS, FEEDFWD_UNITS)
    mlp_out = block_rounded_product(activated, feedfwd_out_weight, N_MLP)
    block_out = (residual + mlp_out).astype(jnp.bfloat16)
    return (block_out, key_pages_out, value_pages_out)
```

```python
import functools

import jax
import jax.numpy as jnp
from jax import lax
from jax.experimental import pallas as pl
from jax.experimental.pallas import tpu as pltpu
from jax.sharding import PartitionSpec as P

HS = 128
ADAPTER_RANK = 16
REQS = 16
PAGE = 128
EPS = 1e-06
MIB = 1024 * 1024
PREFERRED, CHUNK, SPAN, PARTNER_A, PARTNER_B, ORDERS = range(6)
BF16 = jnp.bfloat16
F32 = jnp.float32


def params(mib=48):
    return pltpu.CompilerParams(vmem_limit_bytes=mib * MIB)


SMALL = pl.CostEstimate(flops=0, bytes_accessed=1, transcendentals=0)
SIDE = pl.CostEstimate(flops=0, bytes_accessed=8 * MIB, transcendentals=0)


def exchange(x, axis, mask):
    size = lax.axis_size(axis)
    return lax.ppermute(x, axis, [(i, i ^ mask) for i in range(size)])


def block_offsets(masks):
    offsets = [0]
    for mask in reversed(masks):
        offsets = offsets + [o ^ mask for o in offsets]
    return offsets


def reduce_step(kept, sent, mask):
    rows, width = kept.shape
    half = rows // 2

    def kernel(kept_ref, got_ref, out_ref, next_ref):
        out_ref[...] = kept_ref[:half].astype(F32) + got_ref[:half].astype(F32)
        next_ref[...] = (kept_ref[half:].astype(F32) + got_ref[half:].astype(F32)).astype(BF16)

    return pl.pallas_call(
        kernel,
        out_shape=[jax.ShapeDtypeStruct((half, width), t) for t in (F32, BF16)],
        cost_estimate=SMALL,
        compiler_params=params(),
        name="reduce_step",
    )(kept, exchange(sent, "mlp", mask))


def reduce_rest(kept, sent, masks):
    for mask in masks[:-1]:
        kept, sent = reduce_step(kept, sent, mask)
    return kept, exchange(sent, "mlp", masks[-1])


def gather_most(rows, masks):
    for mask in masks[:0:-1]:
        rows = jnp.concatenate([rows, exchange(rows, "mlp", mask)], axis=0)
    return rows, exchange(rows, "mlp", masks[0])


def out_projection(control, blocks, order, weight, start, width, tile):
    count, rows, depth = blocks.shape
    total = count * rows
    first = start // tile

    def kernel(control_ref, x_ref, w_ref, kept_ref, sent_ref, x_scratch):
        @pl.when(pl.program_id(0) == 0)
        def _():
            for i in range(count):
                at = control_ref[order + i] if isinstance(order, int) else order[i]
                x_scratch[i * rows : (i + 1) * rows, :] = x_ref[at]

        y = jnp.dot(x_scratch[...], w_ref[...], preferred_element_type=F32).astype(BF16)
        kept_ref[...] = y[: total // 2]
        sent_ref[...] = y[total // 2 :]

    half = jax.ShapeDtypeStruct((total // 2, width), BF16)
    return pl.pallas_call(
        kernel,
        grid_spec=pltpu.PrefetchScalarGridSpec(
            num_scalar_prefetch=1,
            grid=(width // tile,),
            in_specs=[
                pl.BlockSpec((count, rows, depth), lambda j, c: (0, 0, 0)),
                pl.BlockSpec((depth, tile), lambda j, c: (0, first + j)),
            ],
            out_specs=[pl.BlockSpec((total // 2, tile), lambda j, c: (0, j))] * 2,
            scratch_shapes=[pltpu.VMEM((total, depth), BF16)],
        ),
        out_shape=[half, half],
        cost_estimate=SMALL,
        compiler_params=params(),
        name="out_projection",
    )(control, blocks, weight)


def norm(hidden, halves, gain, bias, outs_widths):
    rows, width = hidden.shape
    widths = [a.shape[1] for a, _ in halves]
    flat = [x for pair in halves for x in pair]

    def kernel(*refs):
        hidden_ref, gain_ref, bias_ref = refs[:3]
        parts = refs[3 : 3 + len(flat)]
        residual_ref = refs[3 + len(flat)]
        outs = refs[4 + len(flat) :]
        start = 0
        for i, chunk in enumerate(widths):
            cols = slice(start, start + chunk)
            residual_ref[:, cols] = hidden_ref[:, cols].astype(F32) + (
                parts[2 * i][...].astype(F32) + parts[2 * i + 1][...].astype(F32)
            )
            start += chunk
        residual = residual_ref[...]
        centered = residual - jnp.sum(residual, axis=1, keepdims=True) * (1.0 / width)
        var = jnp.sum(centered * centered, axis=1, keepdims=True) * (1.0 / width)
        normed = centered * lax.rsqrt(var + EPS) * gain_ref[...] + bias_ref[...]
        start = 0
        for out, chunk in zip(outs, outs_widths):
            out[...] = normed[:, start : start + chunk].astype(BF16)
            start += chunk

    return pl.pallas_call(
        kernel,
        out_shape=[jax.ShapeDtypeStruct((rows, width), F32)]
        + [jax.ShapeDtypeStruct((rows, chunk), BF16) for chunk in outs_widths],
        cost_estimate=SMALL,
        compiler_params=params(),
        name="norm",
    )(hidden, gain.reshape(1, width), bias.reshape(1, width), *flat)


def feedfwd_in(control, first, second, swap, late, weight, acc=None):
    half, piece = first[1].shape
    total, units = 2 * half, weight.shape[0]
    rows = total // len(swap)
    per = half // rows
    pieces = first[0].shape[1] // piece

    def times(x, w):
        return lax.dot_general(x, w, (((1,), (1,)), ((), ())), preferred_element_type=F32)

    def kernel(control_ref, a0, a1, b0, b1, w_ref, *refs):
        out_ref = refs[-1]

        @pl.when(pl.program_id(0) == 0)
        def _():
            y = times(jnp.concatenate([a0[...], a1[...]], axis=0), w_ref[...])
            out_ref[...] = y if acc is None else refs[0][...] + y

        @pl.when(pl.program_id(0) == 1)
        def _():
            x = [(b0 if i < per else b1)[(i % per) * rows : (i % per + 1) * rows, :] for i in swap]
            out_ref[...] += times(jnp.concatenate(x, axis=0), w_ref[...])

    which = (lambda c: 1 - c[PREFERRED]) if late else (lambda c: c[PREFERRED])
    own = pl.BlockSpec((half, piece), lambda k, c: (0, which(c)))
    got = pl.BlockSpec((half, piece), lambda k, c: (0, 0))
    full = pl.BlockSpec((total, units), lambda k, c: (0, 0))
    return pl.pallas_call(
        kernel,
        grid_spec=pltpu.PrefetchScalarGridSpec(
            num_scalar_prefetch=1,
            grid=(2,),
            in_specs=[own, got, own, got, pl.BlockSpec((units, piece), lambda k, c: (0, k * pieces + which(c)))]
            + ([] if acc is None else [full]),
            out_specs=full,
        ),
        out_shape=jax.ShapeDtypeStruct((total, units), F32),
        cost_estimate=pl.CostEstimate(
            flops=4 * total * piece * units, bytes_accessed=4 * piece * units, transcendentals=0
        ),
        compiler_params=params(),
        name="feedfwd_in",
    )(control, *first, *second, weight, *([] if acc is None else [acc]))


def down_products(control, first, second, groups, down_flat, segment):
    half, piece = first[1].shape
    total, count = 2 * half, groups
    rows = total // count
    per = half // rows
    width = down_flat.shape[1]
    reps = 1
    while (reps * width) % 128:
        reps *= 2
    span = reps * width
    if reps > 1:
        pos = lax.rem(lax.axis_index("mlp"), reps)
        down_flat = jnp.concatenate(
            [jnp.where(pos == i, down_flat, jnp.zeros_like(down_flat)) for i in range(reps)], axis=1
        )
    reqs = REQS
    rank = down_flat.shape[0] // reqs

    def kernel(control_ref, a0, a1, b0, b1, down_ref, segment_ref, out_ref, x_scratch):
        for chunk, order, lower, upper in ((0, ORDERS, a0, a1), (1, ORDERS + groups, b0, b1)):

            @pl.when(control_ref[CHUNK] == chunk)
            def _():
                for i in range(count):
                    start = pl.multiple_of(control_ref[order + i] * rows, rows)
                    x = (lower if i < per else upper)[(i % per) * rows : (i % per + 1) * rows, :]
                    x_scratch[pl.ds(start, rows), :] = x

        every_rank = lax.dot_general(
            down_ref[...], x_scratch[...], (((1,), (1,)), ((), ())), preferred_element_type=F32
        ).reshape(reqs, rank, total)
        chosen = lax.broadcasted_iota(jnp.int32, (reqs, total), 0) == segment_ref[...]
        out_ref[...] = jnp.sum(jnp.where(chosen[:, None, :], every_rank, 0.0), axis=0)

    own = pl.BlockSpec((half, span), lambda k, c: (0, c[PREFERRED] * (piece // span) + c[SPAN]))
    got = pl.BlockSpec((half, span), lambda k, c: (0, c[SPAN]))
    return pl.pallas_call(
        kernel,
        grid_spec=pltpu.PrefetchScalarGridSpec(
            num_scalar_prefetch=1,
            grid=(1,),
            in_specs=[own, got, own, got]
            + [pl.BlockSpec(x.shape, lambda k, c: (0, 0)) for x in (down_flat, segment)],
            out_specs=pl.BlockSpec((rank, total), lambda k, c: (0, 0)),
            scratch_shapes=[pltpu.VMEM((total, span), BF16)],
        ),
        out_shape=jax.ShapeDtypeStruct((rank, total), F32),
        cost_estimate=SMALL,
        compiler_params=params(),
        name="down_products",
    )(control, *first, *second, down_flat, segment)


def preferred(me, groups):
    return lax.rem(me // (groups // 4), 2)


def stack(control, rows, got, key):
    count, width = rows.shape
    piece = width // 2

    def kernel(control_ref, rows_ref, got_ref, out_ref, first_ref, second_ref):
        out_ref[:count, :] = rows_ref[...]
        out_ref[count:, :] = got_ref[...]
        for which in range(2):

            @pl.when(control_ref[key] == which)
            def _():
                for ref, at in ((first_ref, which), (second_ref, 1 - which)):
                    ref[:count, :] = rows_ref[:, at * piece : (at + 1) * piece]
                    ref[count:, :] = got_ref[:, at * piece : (at + 1) * piece]

    def whole(*shape):
        return pl.BlockSpec(shape, lambda j, c: (0, 0))

    return pl.pallas_call(
        kernel,
        grid_spec=pltpu.PrefetchScalarGridSpec(
            num_scalar_prefetch=1,
            grid=(1,),
            in_specs=[whole(count, width)] * 2,
            out_specs=[whole(2 * count, width)] + [whole(2 * count, piece)] * 2,
        ),
        out_shape=[jax.ShapeDtypeStruct((2 * count, w), BF16) for w in (width, piece, piece)],
        cost_estimate=SMALL,
        compiler_params=params(),
        name="stack",
    )(control, rows, got)


def feedfwd_out_first(control, acc, lowrank, segment, up_flat, weight, width, tile, groups):
    total, units = acc.shape
    reqs, rank = REQS, lowrank.shape[0]
    rows = total // groups

    def kernel(control_ref, acc_ref, low_ref, segment_ref, up_ref, w_ref, act_ref, kept_ref, sent_ref, up_scratch):
        @pl.when(pl.program_id(0) == 0)
        def _():
            low = low_ref[...].astype(BF16).astype(F32)
            chosen = lax.broadcasted_iota(jnp.int32, (reqs, total), 0) == segment_ref[...]
            spread = jnp.where(chosen[:, None, :], low[None, :, :], 0.0).reshape(reqs * rank, total)
            up_scratch[...] = lax.dot_general(
                spread.astype(BF16),
                up_ref[...],
                (((0,), (0,)), ((), ())),
                preferred_element_type=F32,
            )
            for i in range(groups):
                here = slice(i * rows, (i + 1) * rows)
                start = pl.multiple_of(control_ref[ORDERS + i] * rows, rows)
                preact = acc_ref[here, :] + up_scratch[pl.ds(start, rows), :]
                act_ref[here, :] = jax.nn.gelu(preact, approximate=True).astype(BF16)

        y = jnp.dot(act_ref[...], w_ref[...], preferred_element_type=F32).astype(BF16)
        kept_ref[...] = y[: total // 2]
        sent_ref[...] = y[total // 2 :]

    half = jax.ShapeDtypeStruct((total // 2, width), BF16)

    def whole(*shape):
        return pl.BlockSpec(shape, lambda j, c: (0,) * len(shape))

    return pl.pallas_call(
        kernel,
        grid_spec=pltpu.PrefetchScalarGridSpec(
            num_scalar_prefetch=1,
            grid=(width // tile,),
            in_specs=[
                whole(total, units),
                whole(rank, total),
                whole(1, total),
                whole(reqs * rank, units),
                pl.BlockSpec((units, tile), lambda j, c: (0, j)),
            ],
            out_specs=[whole(total, units)]
            + [pl.BlockSpec((total // 2, tile), lambda j, c: (0, j))] * 2,
            scratch_shapes=[pltpu.VMEM((total, units), F32)],
        ),
        out_shape=[jax.ShapeDtypeStruct((total, units), BF16), half, half],
        cost_estimate=SMALL,
        compiler_params=params(),
        name="feedfwd_out_first",
    )(control, acc, lowrank, segment, up_flat, weight)


def gather_req(x, masks):
    parts = [x]
    for mask in masks:
        parts = parts + [exchange(part, "req", mask) for part in parts]
    return parts


def pick(held_at, *banks):
    reqs = held_at.shape[0]
    slots, rank = banks[0][0].shape[:2]
    count = len(banks[0])

    def kernel(at_ref, *refs):
        parts = [refs[i * count : (i + 1) * count] for i in range(len(banks))]
        outs = refs[len(banks) * count : -1]
        sems = refs[-1]

        def fetch(i, part, r):
            to = outs[i].at[r * rank : (r + 1) * rank, :]
            return pltpu.make_async_copy(part.at[lax.rem(at_ref[r], slots)], to, sems.at[i, r])

        for r in range(reqs):
            for p in range(count):

                @pl.when(at_ref[r] // slots == p)
                def _():
                    for i in range(len(banks)):
                        fetch(i, parts[i][p], r).start()

        for r in range(reqs):
            for i in range(len(banks)):
                fetch(i, parts[i][0], r).wait()

    return pl.pallas_call(
        kernel,
        grid_spec=pltpu.PrefetchScalarGridSpec(
            num_scalar_prefetch=1,
            grid=(1,),
            in_specs=[pl.BlockSpec(memory_space=pl.ANY)] * (len(banks) * count),
            out_specs=[pl.BlockSpec(memory_space=pl.ANY)] * len(banks),
            scratch_shapes=[pltpu.SemaphoreType.DMA((len(banks), reqs))],
        ),
        out_shape=[jax.ShapeDtypeStruct((reqs * rank, b[0].shape[2]), BF16) for b in banks],
        cost_estimate=SIDE,
        compiler_params=params(),
        name="pick",
    )(held_at, *(part for bank in banks for part in bank))


def join(arrays, groups):
    rows, width = arrays[0].shape
    depth = width // groups

    per = 2
    steps = groups // per

    def kernel(*refs):
        out_ref = refs[-1]
        for i, ref in enumerate(refs[:-1]):
            for g in range(per):
                out_ref[g, :, i * depth : (i + 1) * depth] = ref[:, g * depth : (g + 1) * depth]

    return pl.pallas_call(
        kernel,
        grid=(steps,),
        in_specs=[pl.BlockSpec((rows, per * depth), lambda g: (0, g))] * len(arrays),
        out_specs=pl.BlockSpec((per, rows, len(arrays) * depth), lambda g: (g, 0, 0)),
        out_shape=jax.ShapeDtypeStruct((groups, rows, len(arrays) * depth), BF16),
        cost_estimate=SMALL,
        compiler_params=params(60),
        name="join",
    )(*arrays)


def attend(control, joined, segment, count, weight, width, tile):
    total = joined.shape[0]
    depth = joined.shape[1] // 3
    rows = total // count

    def kernel(control_ref, joined_ref, col_ref, row_ref, w_ref, att_ref, kept_ref, sent_ref, x_scratch):
        @pl.when(pl.program_id(0) == 0)
        def _():
            across = lax.broadcasted_iota(jnp.int32, (total, total), 1)
            down = lax.broadcasted_iota(jnp.int32, (total, total), 0)
            allowed = (col_ref[...] == row_ref[...]) & (across <= down)
            for head in range(depth // HS):
                q, k, v = (
                    joined_ref[:, i * depth + head * HS : i * depth + (head + 1) * HS] for i in range(3)
                )
                scores = lax.dot_general(
                    q, k, (((1,), (1,)), ((), ())), preferred_element_type=F32
                ) * (HS ** (-0.5))
                masked = jnp.where(allowed, scores, -1e30)
                exponent = jnp.exp(masked - jnp.max(masked, axis=1, keepdims=True))
                weights = (exponent / jnp.sum(exponent, axis=1, keepdims=True)).astype(BF16)
                mixed = jnp.dot(weights, v, preferred_element_type=F32).astype(BF16)
                att_ref[:, :, head * HS : (head + 1) * HS] = mixed.reshape(count, rows, HS)
            for i in range(count):
                x_scratch[i * rows : (i + 1) * rows, :] = att_ref[control_ref[ORDERS + i]]

        y = jnp.dot(x_scratch[...], w_ref[...], preferred_element_type=F32).astype(BF16)
        kept_ref[...] = y[: total // 2]
        sent_ref[...] = y[total // 2 :]

    half = jax.ShapeDtypeStruct((total // 2, width), BF16)
    return pl.pallas_call(
        kernel,
        grid_spec=pltpu.PrefetchScalarGridSpec(
            num_scalar_prefetch=1,
            grid=(width // tile,),
            in_specs=[
                pl.BlockSpec((total, 3 * depth), lambda j, o: (0, 0)),
                pl.BlockSpec((total, 1), lambda j, o: (0, 0)),
                pl.BlockSpec((1, total), lambda j, o: (0, 0)),
                pl.BlockSpec((depth, tile), lambda j, o: (0, j)),
            ],
            out_specs=[pl.BlockSpec((count, rows, depth), lambda j, o: (0, 0, 0))]
            + [pl.BlockSpec((total // 2, tile), lambda j, o: (0, j))] * 2,
            scratch_shapes=[pltpu.VMEM((total, depth), BF16)],
        ),
        out_shape=[jax.ShapeDtypeStruct((count, rows, depth), BF16), half, half],
        cost_estimate=SMALL,
        compiler_params=params(),
        name="attend",
    )(control, joined, segment.reshape(total, 1), segment.reshape(1, total), weight)


def write_pages(joined, lookup, key_cache, value_cache):
    pages, page, depth = key_cache.shape
    blocks = lookup.shape[0]
    hits = lookup[None, :] == jnp.arange(pages, dtype=jnp.int32)[:, None]
    source = jnp.sum(jnp.where(hits, jnp.arange(1, blocks + 1, dtype=jnp.int32)[None, :], 0), axis=1) - 1

    def kernel(source_ref, k_ref, v_ref, key_cache_ref, value_cache_ref, key_ref, value_ref):
        fresh = source_ref[pl.program_id(0)] >= 0

        @pl.when(fresh)
        def _():
            key_ref[0] = k_ref[...]
            value_ref[0] = v_ref[...]

        @pl.when(jnp.logical_not(fresh))
        def _():
            key_ref[...] = key_cache_ref[...]
            value_ref[...] = value_cache_ref[...]

    def block(part):
        return pl.BlockSpec((page, depth), lambda p, source: (jnp.maximum(source[p], 0), part))

    paged = pl.BlockSpec((1, page, depth), lambda p, source: (p, 0, 0))
    return pl.pallas_call(
        kernel,
        grid_spec=pltpu.PrefetchScalarGridSpec(
            num_scalar_prefetch=1,
            grid=(pages,),
            in_specs=[block(1), block(2), paged, paged],
            out_specs=[paged, paged],
        ),
        out_shape=[jax.ShapeDtypeStruct(key_cache.shape, BF16)] * 2,
        cost_estimate=SIDE,
        compiler_params=params(),
        name="write_pages",
    )(source, joined, joined, key_cache, value_cache)


def shards(
    queries,
    keys,
    values,
    block_hidden_input,
    attention_out_weight,
    feedfwd_in_weight,
    feedfwd_out_weight,
    norm_gain_vector,
    norm_bias_vector,
    adapter_down_factors,
    adapter_up_factors,
    paged_key_cache,
    paged_value_cache,
    request_prompt_length,
    group_page_lookup,
    adapter_per_request,
    adapter_bank_slot,
):
    tok_rows, width = block_hidden_input.shape
    groups = lax.axis_size("mlp")
    group_rows = tok_rows * groups
    head_cols = attention_out_weight.shape[0]
    me = lax.axis_index("mlp")
    chunk = width // 2
    bits = [1 << i for i in range(groups.bit_length() - 1)]
    minor = len(bits) - 2
    masks_a = bits
    masks_b = bits[minor : minor + 1] + bits[:minor] + bits[minor + 1 :]
    offsets_a, offsets_b = block_offsets(masks_a), block_offsets(masks_b)
    width_dev = width // groups
    control = jnp.concatenate(
        [
            jnp.stack(
                [
                    preferred(me, groups),
                    me // (groups // 2),
                    lax.rem(me, groups // 4) * width_dev // (-(-width_dev // 128) * 128),
                    preferred(me ^ masks_a[0], groups),
                    preferred(me ^ masks_b[0], groups),
                ]
            ),
            jnp.asarray(offsets_a + offsets_b, jnp.int32) ^ me,
        ]
    ).astype(jnp.int32)
    b_of_a = [offsets_b.index(o) for o in offsets_a]
    a_of_b = [offsets_a.index(o) for o in offsets_b]

    req_masks = [1 << i for i in range(lax.axis_size("req").bit_length() - 1)]
    down_bank = gather_req(jnp.swapaxes(adapter_down_factors, 1, 2), req_masks[::-1])
    up_bank = gather_req(adapter_up_factors, req_masks[::-1])
    slots = adapter_down_factors.shape[0]
    adapter_ids = adapter_per_request[0]
    matched = (
        adapter_ids[:, None] == jnp.arange(adapter_bank_slot.shape[0], dtype=jnp.int32)[None, :]
    )
    wanted = jnp.sum(jnp.where(matched, adapter_bank_slot[None, :], 0), axis=1)
    part_owner = jnp.asarray(block_offsets(req_masks), jnp.int32) ^ lax.axis_index("req")
    held_slot = (
        part_owner[:, None] * slots + jnp.arange(slots, dtype=jnp.int32)[None, :]
    ).reshape(-1)
    hit = wanted[:, None] == held_slot[None, :]
    held_at = jnp.sum(jnp.where(hit, jnp.arange(hit.shape[1], dtype=jnp.int32)[None, :], 0), axis=1)

    joined = lax.all_to_all(
        join((queries, keys, values), groups), "mlp", split_axis=0, concat_axis=0, tiled=True
    ).reshape(group_rows, 3 * head_cols)

    wide = width * 3 // 5
    tile = wide // 3
    request_ends = jnp.cumsum(request_prompt_length[0])
    positions = jnp.arange(group_rows, dtype=jnp.int32)
    segment = jnp.sum((positions[:, None] >= request_ends[None, :]).astype(jnp.int32), axis=1)
    joined, segment, control, held_at = lax.optimization_barrier((joined, segment, control, held_at))
    attended, *part_a = attend(control, joined, segment, groups, attention_out_weight, wide, tile)
    part_b = out_projection(
        control, attended, ORDERS + groups, attention_out_weight, wide, width - wide, tile
    )
    kept_b, sent_b = reduce_step(*part_b, masks_b[0])
    kept_a, sent_a = reduce_step(*part_a, masks_a[0])

    sent_a, joined = lax.optimization_barrier((sent_a, joined))
    key_pages_out, value_pages_out = write_pages(
        joined, group_page_lookup[0], paged_key_cache, paged_value_cache
    )
    down_flat, up_flat = pick(held_at, down_bank, up_bank)

    sum_a = reduce_rest(kept_a, sent_a, masks_a[1:])
    sum_b = reduce_rest(kept_b, sent_b, masks_b[1:])
    residual, normed_a, normed_b = norm(
        block_hidden_input, (sum_a, sum_b), norm_gain_vector, norm_bias_vector, (chunk, chunk)
    )
    most_a, most_b = gather_most(normed_a, masks_a[1:]), gather_most(normed_b, masks_b[1:])
    most_a, most_b, down_flat, up_flat, key_pages_out, value_pages_out = lax.optimization_barrier(
        (most_a, most_b, down_flat, up_flat, key_pages_out, value_pages_out)
    )
    half_a, *pieces_a = stack(control, *most_a, PARTNER_A)
    half_b, *pieces_b = stack(control, *most_b, PARTNER_B)
    early_a, early_b = exchange(pieces_a[0], "mlp", masks_a[0]), exchange(pieces_b[0], "mlp", masks_b[0])
    late_a, late_b = exchange(pieces_a[1], "mlp", masks_a[0]), exchange(pieces_b[1], "mlp", masks_b[0])

    early = ((half_a, early_a), (half_b, early_b))
    late = ((half_a, late_a), (half_b, late_b))
    segment = segment.reshape(1, group_rows)
    lowrank = down_products(control, *early, groups, down_flat, segment)
    acc = feedfwd_in(control, *early, b_of_a, False, feedfwd_in_weight.T)
    for mask in bits[:minor]:
        lowrank = lowrank + exchange(lowrank, "mlp", mask)
    lowrank, acc = lax.optimization_barrier((lowrank, acc))
    lowrank = lowrank + sum(exchange(lowrank, "mlp", k << minor) for k in range(1, groups >> minor))
    acc = feedfwd_in(control, *late, b_of_a, True, feedfwd_in_weight.T, acc)

    activated, *part_a = feedfwd_out_first(
        control, acc, lowrank, segment, up_flat, feedfwd_out_weight, wide, tile, groups
    )
    part_b = out_projection(
        control,
        activated.reshape(groups, tok_rows, -1),
        a_of_b,
        feedfwd_out_weight,
        wide,
        width - wide,
        tile,
    )
    sums = (reduce_rest(*part_a, masks_a), reduce_rest(*part_b, masks_b))
    block_out = (
        residual
        + jnp.concatenate([a.astype(F32) + b.astype(F32) for a, b in sums], axis=1)
    ).astype(BF16)
    return (block_out, key_pages_out, value_pages_out)


def solution(mesh):
    in_specs = (
        P(("req", "mlp"), None),
        P(("req", "mlp"), None),
        P(("req", "mlp"), None),
        P(("req", "mlp"), None),
        P("mlp", None),
        P(None, "mlp"),
        P("mlp", None),
        P(),
        P(),
        P("req", "mlp", None),
        P("req", None, "mlp"),
        P("req", None, "mlp"),
        P("req", None, "mlp"),
        P("req", None),
        P("req", None),
        P("req", None),
        P(),
    )
    out_specs = (P(("req", "mlp"), None), P("req", None, "mlp"), P("req", None, "mlp"))
    return jax.shard_map(shards, mesh=mesh, in_specs=in_specs, out_specs=out_specs, check_vma=False)
```

```python
import functools

import jax
import jax.numpy as jnp
from jax import lax
from jax.experimental import pallas as pl
from jax.experimental.pallas import tpu as pltpu
from jax.sharding import PartitionSpec as P

HS = 128
ADAPTER_RANK = 16
REQS = 16
PAGE = 128
EPS = 1e-06
MIB = 1024 * 1024
SPAN, ORDER = range(2)
BF16 = jnp.bfloat16
F32 = jnp.float32


def params(mib=22):
    return pltpu.CompilerParams(vmem_limit_bytes=mib * MIB)


SMALL = pl.CostEstimate(flops=0, bytes_accessed=1, transcendentals=0)
SIDE = pl.CostEstimate(flops=0, bytes_accessed=8 * MIB, transcendentals=0)


def exchange(x, axis, mask):
    size = lax.axis_size(axis)
    return lax.ppermute(x, axis, [(i, i ^ mask) for i in range(size)])


def swap(x, masks):
    reqs, size = lax.axis_size("req"), lax.axis_size("mlp")
    pairs = [
        (r * size + i, r * size + (i ^ masks[r % 2])) for r in range(reqs) for i in range(size)
    ]
    return lax.ppermute(x, ("req", "mlp"), pairs)


def block_offsets(masks):
    offsets = [0]
    for mask in reversed(masks):
        offsets = offsets + [o ^ mask for o in offsets]
    return offsets


def reduce_step(kept, sent, masks):
    rows, width = kept.shape
    half = rows // 2

    def kernel(kept_ref, got_ref, out_ref, next_ref):
        out_ref[...] = kept_ref[:half].astype(F32) + got_ref[:half].astype(F32)
        next_ref[...] = (kept_ref[half:].astype(F32) + got_ref[half:].astype(F32)).astype(BF16)

    return pl.pallas_call(
        kernel,
        out_shape=[jax.ShapeDtypeStruct((half, width), t) for t in (F32, BF16)],
        cost_estimate=SMALL,
        compiler_params=params(16),
        name="reduce_step",
    )(kept, swap(sent, masks))


def reduce_rows(kept, sent, steps):
    for masks in steps[:-1]:
        kept, sent = reduce_step(kept, sent, masks)
    return kept, swap(sent, steps[-1])


def grow(rows, masks, *first):
    return jnp.concatenate([rows, after(swap(rows, masks), *first)], axis=0)


def tied(*values):
    return lax.optimization_barrier(values)


def after(value, *first):
    return tied(value, *first)[0]


def out_projection(control, blocks, part, weight):
    count, rows, depth = blocks.shape
    rows = rows // 2
    total = count * rows
    width = weight.shape[1]
    tile = width // 4

    def kernel(control_ref, x_ref, w_ref, kept_ref, sent_ref, x_scratch):
        @pl.when(pl.program_id(0) == 0)
        def _():
            for i in range(count):
                x = x_ref[control_ref[ORDER + i], part * rows : (part + 1) * rows, :]
                x_scratch[i * rows : (i + 1) * rows, :] = x

        y = jnp.dot(x_scratch[...], w_ref[...], preferred_element_type=F32).astype(BF16)
        kept_ref[...] = y[: total // 2]
        sent_ref[...] = y[total // 2 :]

    half = jax.ShapeDtypeStruct((total // 2, width), BF16)
    return pl.pallas_call(
        kernel,
        grid_spec=pltpu.PrefetchScalarGridSpec(
            num_scalar_prefetch=1,
            grid=(width // tile,),
            in_specs=[
                pl.BlockSpec(blocks.shape, lambda j, c: (0, 0, 0)),
                pl.BlockSpec((depth, tile), lambda j, c: (0, j)),
            ],
            out_specs=[pl.BlockSpec((total // 2, tile), lambda j, c: (0, j))] * 2,
            scratch_shapes=[pltpu.VMEM((total, depth), BF16)],
        ),
        out_shape=[half, half],
        cost_estimate=SMALL,
        compiler_params=params(48),
        name="out_projection",
    )(control, blocks, weight)


def feedfwd_out(activated, weight, start, width, tile):
    total, depth = activated.shape
    first = start // tile

    def kernel(x_ref, w_ref, kept_ref, sent_ref):
        y = jnp.dot(x_ref[...], w_ref[...], preferred_element_type=F32).astype(BF16)
        kept_ref[...] = y[: total // 2]
        sent_ref[...] = y[total // 2 :]

    half = jax.ShapeDtypeStruct((total // 2, width), BF16)
    return pl.pallas_call(
        kernel,
        grid=(width // tile,),
        in_specs=[
            pl.BlockSpec((total, depth), lambda j: (0, 0)),
            pl.BlockSpec((depth, tile), lambda j: (0, first + j)),
        ],
        out_specs=[pl.BlockSpec((total // 2, tile), lambda j: (0, j))] * 2,
        out_shape=[half, half],
        cost_estimate=SMALL,
        compiler_params=params(),
        name="feedfwd_out",
    )(activated, weight)


def norm(hidden, part, sums, gain, bias):
    width = hidden.shape[1]
    rows = hidden.shape[0] // 2

    def kernel(hidden_ref, a_ref, b_ref, gain_ref, bias_ref, residual_ref, out_ref):
        residual = hidden_ref[part * rows : (part + 1) * rows, :].astype(F32) + (
            a_ref[...].astype(F32) + b_ref[...].astype(F32)
        )
        residual_ref[...] = residual
        centered = residual - jnp.sum(residual, axis=1, keepdims=True) * (1.0 / width)
        var = jnp.sum(centered * centered, axis=1, keepdims=True) * (1.0 / width)
        out_ref[...] = (centered * lax.rsqrt(var + EPS) * gain_ref[...] + bias_ref[...]).astype(BF16)

    return pl.pallas_call(
        kernel,
        out_shape=[jax.ShapeDtypeStruct((rows, width), t) for t in (F32, BF16)],
        cost_estimate=SMALL,
        compiler_params=params(16),
        name="norm",
    )(hidden, *sums, gain.reshape(1, width), bias.reshape(1, width))


def streamed(weight):
    return pltpu.with_memory_space_constraint(weight, pltpu.HBM)


def feedfwd_in(parts, weight, which, accs=()):
    half, width = parts[0][0].shape
    units = weight.shape[0]
    count = len(parts)
    steps = 2
    piece = width // (2 * steps)

    def kernel(*refs):
        rows, w_ref = refs[: 2 * count], refs[2 * count]
        acc_refs, outs = refs[2 * count + 1 : -count], refs[-count:]
        x = jnp.concatenate([ref[...] for ref in rows], axis=0)
        y = lax.dot_general(x, w_ref[...], (((1,), (1,)), ((), ())), preferred_element_type=F32)

        @pl.when(pl.program_id(0) == 0)
        def _():
            for i, out_ref in enumerate(outs):
                here = y[2 * half * i : 2 * half * (i + 1)]
                out_ref[...] = acc_refs[i][...] + here if acc_refs else here

        @pl.when(pl.program_id(0) > 0)
        def _():
            for i, out_ref in enumerate(outs):
                out_ref[...] += y[2 * half * i : 2 * half * (i + 1)]

    rows = pl.BlockSpec((half, piece), lambda k: (0, which * steps + k))
    full = pl.BlockSpec((2 * half, units), lambda k: (0, 0))
    return pl.pallas_call(
        kernel,
        grid=(steps,),
        in_specs=[rows] * (2 * count)
        + [pl.BlockSpec((units, piece), lambda k: (0, which * steps + k))]
        + [full] * len(accs),
        out_specs=[full] * count,
        out_shape=[jax.ShapeDtypeStruct((2 * half, units), F32)] * count,
        cost_estimate=pl.CostEstimate(
            flops=4 * count * steps * half * piece * units,
            bytes_accessed=2 * steps * piece * units,
            transcendentals=0,
        ),
        compiler_params=params(24),
        name="feedfwd_in",
    )(*(x for part in parts for x in part), streamed(weight), *accs)


def down_products(control, upper, lower, groups, down_flat, segment):
    half = upper.shape[0]
    total = 2 * half
    rows = total // groups
    per = groups // 2
    width = down_flat.shape[1]
    reps = 1
    while (reps * width) % 128:
        reps *= 2
    span = reps * width
    if reps > 1:
        pos = lax.rem(lax.axis_index("mlp"), reps)
        down_flat = jnp.concatenate(
            [jnp.where(pos == i, down_flat, jnp.zeros_like(down_flat)) for i in range(reps)], axis=1
        )
    reqs = REQS
    rank = down_flat.shape[0] // reqs

    def kernel(control_ref, a_ref, b_ref, down_ref, segment_ref, out_ref, x_scratch):
        for i in range(groups):
            start = pl.multiple_of(control_ref[ORDER + i] * rows, rows)
            x = (a_ref if i < per else b_ref)[(i % per) * rows : (i % per + 1) * rows, :]
            x_scratch[pl.ds(start, rows), :] = x

        every_rank = lax.dot_general(
            down_ref[...], x_scratch[...], (((1,), (1,)), ((), ())), preferred_element_type=F32
        ).reshape(reqs, rank, total)
        chosen = lax.broadcasted_iota(jnp.int32, (reqs, total), 0) == segment_ref[...]
        out_ref[...] = jnp.sum(jnp.where(chosen[:, None, :], every_rank, 0.0), axis=0)

    own = pl.BlockSpec((half, span), lambda k, c: (0, c[SPAN]))
    return pl.pallas_call(
        kernel,
        grid_spec=pltpu.PrefetchScalarGridSpec(
            num_scalar_prefetch=1,
            grid=(1,),
            in_specs=[own, own]
            + [pl.BlockSpec(x.shape, lambda k, c: (0, 0)) for x in (down_flat, segment)],
            out_specs=pl.BlockSpec((rank, total), lambda k, c: (0, 0)),
            scratch_shapes=[pltpu.VMEM((total, span), BF16)],
        ),
        out_shape=jax.ShapeDtypeStruct((rank, total), F32),
        cost_estimate=SMALL,
        compiler_params=params(16),
        name="down_products",
    )(control, upper, lower, down_flat, segment)


def feedfwd_out_first(control, accs, lowrank, segments, up_flat, weight, width, tile, groups):
    count, units = accs[0].shape
    parts = len(accs)
    total = parts * count
    reqs, rank = REQS, lowrank.shape[0]
    rows = count // groups

    def kernel(control_ref, *refs):
        acc_refs, segment_refs = (refs[i * parts : (i + 1) * parts] for i in range(2))
        low_ref, up_ref, w_ref, act_ref, kept_ref, sent_ref, up_scratch = refs[2 * parts :]

        @pl.when(pl.program_id(0) == 0)
        def _():
            spreads = []
            for part, segment_ref in enumerate(segment_refs):
                low = low_ref[:, part * count : (part + 1) * count].astype(BF16).astype(F32)
                chosen = lax.broadcasted_iota(jnp.int32, (reqs, count), 0) == segment_ref[...]
                spread = jnp.where(chosen[:, None, :], low[None, :, :], 0.0)
                spreads.append(spread.reshape(reqs * rank, count).astype(BF16))
            up_scratch[...] = lax.dot_general(
                jnp.concatenate(spreads, axis=1),
                up_ref[...],
                (((0,), (0,)), ((), ())),
                preferred_element_type=F32,
            )
            for i in range(groups):
                for part, acc_ref in enumerate(acc_refs):
                    start = pl.multiple_of(part * count + control_ref[ORDER + i] * rows, rows)
                    preact = acc_ref[i * rows : (i + 1) * rows, :] + up_scratch[pl.ds(start, rows), :]
                    here = (i * parts + part) * rows
                    act_ref[here : here + rows, :] = jax.nn.gelu(preact, approximate=True).astype(BF16)

        y = jnp.dot(act_ref[...], w_ref[...], preferred_element_type=F32).astype(BF16)
        kept_ref[...] = y[: total // 2]
        sent_ref[...] = y[total // 2 :]

    half = jax.ShapeDtypeStruct((total // 2, width), BF16)

    def whole(*shape):
        return pl.BlockSpec(shape, lambda j, c: (0,) * len(shape))

    return pl.pallas_call(
        kernel,
        grid_spec=pltpu.PrefetchScalarGridSpec(
            num_scalar_prefetch=1,
            grid=(width // tile,),
            in_specs=[whole(count, units)] * parts
            + [whole(1, count)] * parts
            + [whole(rank, total), whole(reqs * rank, units), pl.BlockSpec((units, tile), lambda j, c: (0, j))],
            out_specs=[whole(total, units)]
            + [pl.BlockSpec((total // 2, tile), lambda j, c: (0, j))] * 2,
            scratch_shapes=[pltpu.VMEM((total, units), F32)],
        ),
        out_shape=[jax.ShapeDtypeStruct((total, units), BF16), half, half],
        cost_estimate=SMALL,
        compiler_params=params(),
        name="feedfwd_out_first",
    )(control, *accs, *segments, lowrank, up_flat, weight)


def pick(held_at, *banks):
    reqs = held_at.shape[0]
    slots, rank = banks[0][0].shape[:2]
    count = len(banks[0])

    def kernel(at_ref, *refs):
        parts = [refs[i * count : (i + 1) * count] for i in range(len(banks))]
        outs = refs[len(banks) * count : -1]
        sems = refs[-1]

        def fetch(i, part, r):
            to = outs[i].at[r * rank : (r + 1) * rank, :]
            return pltpu.make_async_copy(part.at[lax.rem(at_ref[r], slots)], to, sems.at[i, r])

        for r in range(reqs):
            for p in range(count):

                @pl.when(at_ref[r] // slots == p)
                def _():
                    for i in range(len(banks)):
                        fetch(i, parts[i][p], r).start()

        for r in range(reqs):
            for i in range(len(banks)):
                fetch(i, parts[i][0], r).wait()

    return pl.pallas_call(
        kernel,
        grid_spec=pltpu.PrefetchScalarGridSpec(
            num_scalar_prefetch=1,
            grid=(1,),
            in_specs=[pl.BlockSpec(memory_space=pl.ANY)] * (len(banks) * count),
            out_specs=[pl.BlockSpec(memory_space=pl.ANY)] * len(banks),
            scratch_shapes=[pltpu.SemaphoreType.DMA((len(banks), reqs))],
        ),
        out_shape=[jax.ShapeDtypeStruct((reqs * rank, b[0].shape[2]), BF16) for b in banks],
        cost_estimate=SIDE,
        compiler_params=params(16),
        name="pick",
    )(held_at, *(part for bank in banks for part in bank))


def join(arrays, groups):
    rows, width = arrays[0].shape
    depth = width // groups

    per = 2
    steps = groups // per

    def kernel(*refs):
        out_ref = refs[-1]
        for i, ref in enumerate(refs[:-1]):
            for g in range(per):
                out_ref[g, :, i * depth : (i + 1) * depth] = ref[:, g * depth : (g + 1) * depth]

    return pl.pallas_call(
        kernel,
        grid=(steps,),
        in_specs=[pl.BlockSpec((rows, per * depth), lambda g: (0, g))] * len(arrays),
        out_specs=pl.BlockSpec((per, rows, len(arrays) * depth), lambda g: (g, 0, 0)),
        out_shape=jax.ShapeDtypeStruct((groups, rows, len(arrays) * depth), BF16),
        cost_estimate=SMALL,
        compiler_params=params(60),
        name="join",
    )(*arrays)


def attend(control, joined, segment, count, weight):
    total = joined.shape[0]
    depth = joined.shape[1] // 3
    rows = total // count
    first = rows // 2
    width = weight.shape[1]
    tile = width // 4

    def kernel(control_ref, joined_ref, col_ref, row_ref, w_ref, att_ref, kept_ref, sent_ref, x_scratch):
        @pl.when(pl.program_id(0) == 0)
        def _():
            across = lax.broadcasted_iota(jnp.int32, (total, total), 1)
            down = lax.broadcasted_iota(jnp.int32, (total, total), 0)
            allowed = (col_ref[...] == row_ref[...]) & (across <= down)
            for head in range(depth // HS):
                q, k, v = (
                    joined_ref[:, i * depth + head * HS : i * depth + (head + 1) * HS] for i in range(3)
                )
                scores = lax.dot_general(
                    q, k, (((1,), (1,)), ((), ())), preferred_element_type=F32
                ) * (HS ** (-0.5))
                masked = jnp.where(allowed, scores, -1e30)
                exponent = jnp.exp(masked - jnp.max(masked, axis=1, keepdims=True))
                weights = (exponent / jnp.sum(exponent, axis=1, keepdims=True)).astype(BF16)
                mixed = jnp.dot(weights, v, preferred_element_type=F32).astype(BF16)
                att_ref[:, :, head * HS : (head + 1) * HS] = mixed.reshape(count, rows, HS)
            for i in range(count):
                x_scratch[i * first : (i + 1) * first, :] = att_ref[control_ref[ORDER + i], :first, :]

        y = jnp.dot(x_scratch[...], w_ref[...], preferred_element_type=F32).astype(BF16)
        kept_ref[...] = y[: total // 4]
        sent_ref[...] = y[total // 4 :]

    half = jax.ShapeDtypeStruct((total // 4, width), BF16)
    return pl.pallas_call(
        kernel,
        grid_spec=pltpu.PrefetchScalarGridSpec(
            num_scalar_prefetch=1,
            grid=(width // tile,),
            in_specs=[
                pl.BlockSpec((total, 3 * depth), lambda j, o: (0, 0)),
                pl.BlockSpec((total, 1), lambda j, o: (0, 0)),
                pl.BlockSpec((1, total), lambda j, o: (0, 0)),
                pl.BlockSpec((depth, tile), lambda j, o: (0, j)),
            ],
            out_specs=[pl.BlockSpec((count, rows, depth), lambda j, o: (0, 0, 0))]
            + [pl.BlockSpec((total // 4, tile), lambda j, o: (0, j))] * 2,
            scratch_shapes=[pltpu.VMEM((total // 2, depth), BF16)],
        ),
        out_shape=[jax.ShapeDtypeStruct((count, rows, depth), BF16), half, half],
        cost_estimate=SMALL,
        compiler_params=params(48),
        name="attend",
    )(control, joined, segment.reshape(total, 1), segment.reshape(1, total), weight)


def write_pages(joined, lookup, key_cache, value_cache):
    pages, page, depth = key_cache.shape
    blocks = lookup.shape[0]
    hits = lookup[None, :] == jnp.arange(pages, dtype=jnp.int32)[:, None]
    source = jnp.sum(jnp.where(hits, jnp.arange(1, blocks + 1, dtype=jnp.int32)[None, :], 0), axis=1) - 1

    def kernel(source_ref, k_ref, v_ref, key_cache_ref, value_cache_ref, key_ref, value_ref):
        fresh = source_ref[pl.program_id(0)] >= 0

        @pl.when(fresh)
        def _():
            key_ref[0] = k_ref[...]
            value_ref[0] = v_ref[...]

        @pl.when(jnp.logical_not(fresh))
        def _():
            key_ref[...] = key_cache_ref[...]
            value_ref[...] = value_cache_ref[...]

    def block(part):
        return pl.BlockSpec((page, depth), lambda p, source: (jnp.maximum(source[p], 0), part))

    paged = pl.BlockSpec((1, page, depth), lambda p, source: (p, 0, 0))
    return pl.pallas_call(
        kernel,
        grid_spec=pltpu.PrefetchScalarGridSpec(
            num_scalar_prefetch=1,
            grid=(pages,),
            in_specs=[block(1), block(2), paged, paged],
            out_specs=[paged, paged],
        ),
        out_shape=[jax.ShapeDtypeStruct(key_cache.shape, BF16)] * 2,
        cost_estimate=SIDE,
        compiler_params=params(16),
        name="write_pages",
    )(source, joined, joined, key_cache, value_cache)


def shards(
    queries,
    keys,
    values,
    block_hidden_input,
    attention_out_weight,
    feedfwd_in_weight,
    feedfwd_out_weight,
    norm_gain_vector,
    norm_bias_vector,
    adapter_down_factors,
    adapter_up_factors,
    paged_key_cache,
    paged_value_cache,
    request_prompt_length,
    group_page_lookup,
    adapter_per_request,
    adapter_bank_slot,
):
    tok_rows, width = block_hidden_input.shape
    groups = lax.axis_size("mlp")
    group_rows = tok_rows * groups
    head_cols = attention_out_weight.shape[0]
    me = lax.axis_index("mlp")
    bits = [1 << i for i in range(groups.bit_length() - 1)]
    minor = len(bits) - 2
    orders = bits, bits[minor : minor + 1] + bits[:minor] + bits[minor + 1 :]
    steps = list(zip(*orders))
    width_dev = width // groups
    span = width_dev
    while span % 128:
        span *= 2
    first_core = lax.rem(lax.axis_index("req"), 2) == 0
    offsets = [jnp.asarray(block_offsets(masks), jnp.int32) for masks in orders]
    control = jnp.concatenate(
        [jnp.reshape(me * width_dev // span, (1,)), jnp.where(first_core, *offsets) ^ me]
    ).astype(jnp.int32)

    req_masks = [1 << i for i in range(lax.axis_size("req").bit_length() - 1)]
    banks = jnp.swapaxes(adapter_down_factors, 1, 2), adapter_up_factors
    banks = [[x, exchange(x, "req", req_masks[-1])] for x in banks]
    slots = adapter_down_factors.shape[0]
    adapter_ids = adapter_per_request[0]
    matched = (
        adapter_ids[:, None] == jnp.arange(adapter_bank_slot.shape[0], dtype=jnp.int32)[None, :]
    )
    wanted = jnp.sum(jnp.where(matched, adapter_bank_slot[None, :], 0), axis=1)
    part_owner = jnp.asarray(block_offsets(req_masks), jnp.int32) ^ lax.axis_index("req")
    held_slot = (
        part_owner[:, None] * slots + jnp.arange(slots, dtype=jnp.int32)[None, :]
    ).reshape(-1)
    hit = wanted[:, None] == held_slot[None, :]
    held_at = jnp.sum(jnp.where(hit, jnp.arange(hit.shape[1], dtype=jnp.int32)[None, :], 0), axis=1)

    joined = lax.all_to_all(
        join((queries, keys, values), groups), "mlp", split_axis=0, concat_axis=0, tiled=True
    ).reshape(group_rows, 3 * head_cols)

    request_ends = jnp.cumsum(request_prompt_length[0])
    positions = jnp.arange(group_rows, dtype=jnp.int32)
    segment = jnp.sum((positions[:, None] >= request_ends[None, :]).astype(jnp.int32), axis=1)
    joined, segment, control, held_at = tied(joined, segment, control, held_at)
    attended, *partial_a = attend(control, joined, segment, groups, attention_out_weight)
    partial_b = out_projection(control, attended, 1, attention_out_weight)
    kept_a, sent_a = reduce_step(*partial_a, steps[0])

    sent_a, joined, banks = tied(sent_a, joined, banks)
    for mask in req_masks[-2::-1]:
        banks = [parts + [exchange(part, "req", mask) for part in parts] for parts in banks]
    pages_out = write_pages(joined, group_page_lookup[0], paged_key_cache, paged_value_cache)
    factors = pick(held_at, *banks)

    vectors = norm_gain_vector, norm_bias_vector
    residual_a, rows_a = norm(
        block_hidden_input, 0, reduce_rows(kept_a, sent_a, steps[1:]), *vectors
    )
    rows_a = grow(rows_a, steps[-1])
    sum_b, (key_pages_out, value_pages_out), (down_flat, up_flat), _ = tied(
        reduce_rows(*partial_b, steps), pages_out, factors, rows_a
    )
    residual_b, rows_b = norm(block_hidden_input, 1, sum_b, *vectors)
    ahead = steps[-2::-1]
    for masks, masks_ahead in zip(steps[:0:-1], ahead):
        if masks_ahead is steps[0]:
            rows_a = rows_a, swap(rows_a, masks_ahead)
            rows_b = grow(rows_b, masks, rows_a[1])
        else:
            rows_a = grow(rows_a, masks_ahead)
            rows_b = grow(rows_b, masks, rows_a)
    rows_b = rows_b, swap(rows_b, steps[0])

    part_rows = tok_rows // 2
    segments = [
        segment.reshape(groups, 2, part_rows)[:, part].reshape(1, groups * part_rows)
        for part in range(2)
    ]
    win = feedfwd_in_weight.T
    low_a = down_products(control, *rows_a, groups, down_flat, segments[0])
    acc_a = feedfwd_in([rows_a], win, 0)
    rows_b, low_a, acc_a = tied(rows_b, low_a, acc_a)
    low_b = down_products(control, *rows_b, groups, down_flat, segments[1])
    lowrank = jnp.concatenate([low_a, low_b], axis=1)
    acc_b = feedfwd_in([rows_b], win, 0)
    for mask in bits[:minor]:
        lowrank = lowrank + exchange(lowrank, "mlp", mask)
    lowrank, acc_b = tied(lowrank, acc_b)
    lowrank = lowrank + sum(
        exchange(lowrank, "mlp", k << minor) for k in range(1, groups >> minor)
    )
    acc = feedfwd_in([rows_a, rows_b], win, 1, acc_a + acc_b)

    wide = width * 3 // 5
    tile = wide // 3
    activated, *partial_a = feedfwd_out_first(
        control, acc, lowrank, segments, up_flat, feedfwd_out_weight, wide, tile, groups
    )
    partial_b = feedfwd_out(activated, feedfwd_out_weight, wide, width - wide, tile)
    partial_a = reduce_step(*partial_a, steps[0])
    partial_a, partial_b = tied(partial_a, partial_b)
    partial_b = reduce_step(*partial_b, steps[0])
    for masks in steps[1:-1]:
        partial_a = reduce_step(*partial_a, masks)
        partial_a, partial_b = tied(partial_a, partial_b)
        partial_b = reduce_step(*partial_b, masks)
    sums = (
        (partial_a[0], swap(partial_a[1], steps[-1])),
        (partial_b[0], swap(partial_b[1], steps[-1])),
    )
    block_out = (
        jnp.concatenate([residual_a, residual_b], axis=0)
        + jnp.concatenate([a.astype(F32) + b.astype(F32) for a, b in sums], axis=1)
    ).astype(BF16)
    return (block_out, key_pages_out, value_pages_out)


def solution(mesh):
    in_specs = (
        P(("req", "mlp"), None),
        P(("req", "mlp"), None),
        P(("req", "mlp"), None),
        P(("req", "mlp"), None),
        P("mlp", None),
        P(None, "mlp"),
        P("mlp", None),
        P(),
        P(),
        P("req", "mlp", None),
        P("req", None, "mlp"),
        P("req", None, "mlp"),
        P("req", None, "mlp"),
        P("req", None),
        P("req", None),
        P("req", None),
        P(),
    )
    out_specs = (P(("req", "mlp"), None), P("req", None, "mlp"), P("req", None, "mlp"))
    return jax.shard_map(shards, mesh=mesh, in_specs=in_specs, out_specs=out_specs, check_vma=False)
```

```python
import functools

import jax
import jax.numpy as jnp
from jax import lax
from jax.experimental import pallas as pl
from jax.experimental.pallas import tpu as pltpu
from jax.sharding import PartitionSpec as P

HS = 128
ADAPTER_RANK = 16
REQS = 16
PAGE = 128
EPS = 1e-06
MIB = 1024 * 1024
SPAN, ORDER = range(2)
BF16 = jnp.bfloat16
F32 = jnp.float32


def params(mib=22):
    return pltpu.CompilerParams(vmem_limit_bytes=mib * MIB)


SMALL = pl.CostEstimate(flops=0, bytes_accessed=1, transcendentals=0)
SIDE = pl.CostEstimate(flops=0, bytes_accessed=8 * MIB, transcendentals=0)


def exchange(x, axis, mask):
    size = lax.axis_size(axis)
    return lax.ppermute(x, axis, [(i, i ^ mask) for i in range(size)])


def swap(x, masks):
    reqs, size = lax.axis_size("req"), lax.axis_size("mlp")
    pairs = [
        (r * size + i, r * size + (i ^ masks[r % 2])) for r in range(reqs) for i in range(size)
    ]
    return lax.ppermute(x, ("req", "mlp"), pairs)


def block_offsets(masks):
    offsets = [0]
    for mask in reversed(masks):
        offsets = offsets + [o ^ mask for o in offsets]
    return offsets


def reduce_step(kept, sent, masks):
    rows, width = kept.shape
    half = rows // 2

    def kernel(kept_ref, got_ref, out_ref, next_ref):
        out_ref[...] = kept_ref[:half].astype(F32) + got_ref[:half].astype(F32)
        next_ref[...] = (kept_ref[half:].astype(F32) + got_ref[half:].astype(F32)).astype(BF16)

    return pl.pallas_call(
        kernel,
        out_shape=[jax.ShapeDtypeStruct((half, width), t) for t in (F32, BF16)],
        cost_estimate=SMALL,
        compiler_params=params(16),
        name="reduce_step",
    )(kept, swap(sent, masks))


def reduce_rows(kept, sent, steps):
    for masks in steps[:-1]:
        kept, sent = reduce_step(kept, sent, masks)
    return kept, swap(sent, steps[-1])


def grow(rows, masks, *first):
    return jnp.concatenate([rows, after(swap(rows, masks), *first)], axis=0)


def tied(*values):
    return lax.optimization_barrier(values)


def after(value, *first):
    return tied(value, *first)[0]


def out_projection(control, blocks, part, weight):
    count, rows, depth = blocks.shape
    rows = rows // 2
    total = count * rows
    width = weight.shape[1]
    tile = width // 4

    def kernel(control_ref, x_ref, w_ref, kept_ref, sent_ref, x_scratch):
        @pl.when(pl.program_id(0) == 0)
        def _():
            for i in range(count):
                x = x_ref[control_ref[ORDER + i], part * rows : (part + 1) * rows, :]
                x_scratch[i * rows : (i + 1) * rows, :] = x

        y = jnp.dot(x_scratch[...], w_ref[...], preferred_element_type=F32).astype(BF16)
        kept_ref[...] = y[: total // 2]
        sent_ref[...] = y[total // 2 :]

    half = jax.ShapeDtypeStruct((total // 2, width), BF16)
    return pl.pallas_call(
        kernel,
        grid_spec=pltpu.PrefetchScalarGridSpec(
            num_scalar_prefetch=1,
            grid=(width // tile,),
            in_specs=[
                pl.BlockSpec(blocks.shape, lambda j, c: (0, 0, 0)),
                pl.BlockSpec((depth, tile), lambda j, c: (0, j)),
            ],
            out_specs=[pl.BlockSpec((total // 2, tile), lambda j, c: (0, j))] * 2,
            scratch_shapes=[pltpu.VMEM((total, depth), BF16)],
        ),
        out_shape=[half, half],
        cost_estimate=SMALL,
        compiler_params=params(48),
        name="out_projection",
    )(control, blocks, weight)


def feedfwd_out(activated, weight, start, width, tile):
    total, depth = activated.shape
    first = start // tile

    def kernel(x_ref, w_ref, kept_ref, sent_ref):
        y = jnp.dot(x_ref[...], w_ref[...], preferred_element_type=F32).astype(BF16)
        kept_ref[...] = y[: total // 2]
        sent_ref[...] = y[total // 2 :]

    half = jax.ShapeDtypeStruct((total // 2, width), BF16)
    return pl.pallas_call(
        kernel,
        grid=(width // tile,),
        in_specs=[
            pl.BlockSpec((total, depth), lambda j: (0, 0)),
            pl.BlockSpec((depth, tile), lambda j: (0, first + j)),
        ],
        out_specs=[pl.BlockSpec((total // 2, tile), lambda j: (0, j))] * 2,
        out_shape=[half, half],
        cost_estimate=SMALL,
        compiler_params=params(),
        name="feedfwd_out",
    )(activated, weight)


def norm(hidden, part, sums, gain, bias):
    width = hidden.shape[1]
    rows = hidden.shape[0] // 2

    def kernel(hidden_ref, a_ref, b_ref, gain_ref, bias_ref, residual_ref, out_ref):
        residual = hidden_ref[part * rows : (part + 1) * rows, :].astype(F32) + (
            a_ref[...].astype(F32) + b_ref[...].astype(F32)
        )
        residual_ref[...] = residual
        centered = residual - jnp.sum(residual, axis=1, keepdims=True) * (1.0 / width)
        var = jnp.sum(centered * centered, axis=1, keepdims=True) * (1.0 / width)
        out_ref[...] = (centered * lax.rsqrt(var + EPS) * gain_ref[...] + bias_ref[...]).astype(BF16)

    return pl.pallas_call(
        kernel,
        out_shape=[jax.ShapeDtypeStruct((rows, width), t) for t in (F32, BF16)],
        cost_estimate=SMALL,
        compiler_params=params(16),
        name="norm",
    )(hidden, *sums, gain.reshape(1, width), bias.reshape(1, width))


def streamed(weight):
    return pltpu.with_memory_space_constraint(weight, pltpu.HBM)


def feedfwd_in(parts, weight, which, accs=()):
    half, width = parts[0][0].shape
    units = weight.shape[0]
    count = len(parts)
    steps = 2
    piece = width // (2 * steps)

    def kernel(*refs):
        rows, w_ref = refs[: 2 * count], refs[2 * count]
        acc_refs, outs = refs[2 * count + 1 : -count], refs[-count:]
        x = jnp.concatenate([ref[...] for ref in rows], axis=0)
        y = lax.dot_general(x, w_ref[...], (((1,), (1,)), ((), ())), preferred_element_type=F32)

        @pl.when(pl.program_id(0) == 0)
        def _():
            for i, out_ref in enumerate(outs):
                here = y[2 * half * i : 2 * half * (i + 1)]
                out_ref[...] = acc_refs[i][...] + here if acc_refs else here

        @pl.when(pl.program_id(0) > 0)
        def _():
            for i, out_ref in enumerate(outs):
                out_ref[...] += y[2 * half * i : 2 * half * (i + 1)]

    rows = pl.BlockSpec((half, piece), lambda k: (0, which * steps + k))
    full = pl.BlockSpec((2 * half, units), lambda k: (0, 0))
    return pl.pallas_call(
        kernel,
        grid=(steps,),
        in_specs=[rows] * (2 * count)
        + [pl.BlockSpec((units, piece), lambda k: (0, which * steps + k))]
        + [full] * len(accs),
        out_specs=[full] * count,
        out_shape=[jax.ShapeDtypeStruct((2 * half, units), F32)] * count,
        cost_estimate=pl.CostEstimate(
            flops=4 * count * steps * half * piece * units,
            bytes_accessed=2 * steps * piece * units,
            transcendentals=0,
        ),
        compiler_params=params(24),
        name="feedfwd_in",
    )(*(x for part in parts for x in part), streamed(weight), *accs)


def down_products(control, upper, lower, groups, down_flat, segment):
    half = upper.shape[0]
    total = 2 * half
    rows = total // groups
    per = groups // 2
    width = down_flat.shape[1]
    reps = 1
    while (reps * width) % 128:
        reps *= 2
    span = reps * width
    if reps > 1:
        pos = lax.rem(lax.axis_index("mlp"), reps)
        down_flat = jnp.concatenate(
            [jnp.where(pos == i, down_flat, jnp.zeros_like(down_flat)) for i in range(reps)], axis=1
        )
    reqs = REQS
    rank = down_flat.shape[0] // reqs

    def kernel(control_ref, a_ref, b_ref, down_ref, segment_ref, out_ref, x_scratch):
        for i in range(groups):
            start = pl.multiple_of(control_ref[ORDER + i] * rows, rows)
            x = (a_ref if i < per else b_ref)[(i % per) * rows : (i % per + 1) * rows, :]
            x_scratch[pl.ds(start, rows), :] = x

        every_rank = lax.dot_general(
            down_ref[...], x_scratch[...], (((1,), (1,)), ((), ())), preferred_element_type=F32
        ).reshape(reqs, rank, total)
        chosen = lax.broadcasted_iota(jnp.int32, (reqs, total), 0) == segment_ref[...]
        out_ref[...] = jnp.sum(jnp.where(chosen[:, None, :], every_rank, 0.0), axis=0)

    own = pl.BlockSpec((half, span), lambda k, c: (0, c[SPAN]))
    return pl.pallas_call(
        kernel,
        grid_spec=pltpu.PrefetchScalarGridSpec(
            num_scalar_prefetch=1,
            grid=(1,),
            in_specs=[own, own]
            + [pl.BlockSpec(x.shape, lambda k, c: (0, 0)) for x in (down_flat, segment)],
            out_specs=pl.BlockSpec((rank, total), lambda k, c: (0, 0)),
            scratch_shapes=[pltpu.VMEM((total, span), BF16)],
        ),
        out_shape=jax.ShapeDtypeStruct((rank, total), F32),
        cost_estimate=SMALL,
        compiler_params=params(16),
        name="down_products",
    )(control, upper, lower, down_flat, segment)


def feedfwd_out_first(control, accs, lowrank, segments, up_flat, weight, width, tile, groups):
    count, units = accs[0].shape
    parts = len(accs)
    total = parts * count
    reqs, rank = REQS, lowrank.shape[0]
    rows = count // groups

    def kernel(control_ref, *refs):
        acc_refs, segment_refs = (refs[i * parts : (i + 1) * parts] for i in range(2))
        low_ref, up_ref, w_ref, act_ref, kept_ref, sent_ref, up_scratch = refs[2 * parts :]

        @pl.when(pl.program_id(0) == 0)
        def _():
            spreads = []
            for part, segment_ref in enumerate(segment_refs):
                low = low_ref[:, part * count : (part + 1) * count].astype(BF16).astype(F32)
                chosen = lax.broadcasted_iota(jnp.int32, (reqs, count), 0) == segment_ref[...]
                spread = jnp.where(chosen[:, None, :], low[None, :, :], 0.0)
                spreads.append(spread.reshape(reqs * rank, count).astype(BF16))
            up_scratch[...] = lax.dot_general(
                jnp.concatenate(spreads, axis=1),
                up_ref[...],
                (((0,), (0,)), ((), ())),
                preferred_element_type=F32,
            )
            for i in range(groups):
                for part, acc_ref in enumerate(acc_refs):
                    start = pl.multiple_of(part * count + control_ref[ORDER + i] * rows, rows)
                    preact = acc_ref[i * rows : (i + 1) * rows, :] + up_scratch[pl.ds(start, rows), :]
                    here = (i * parts + part) * rows
                    act_ref[here : here + rows, :] = jax.nn.gelu(preact, approximate=True).astype(BF16)

        y = jnp.dot(act_ref[...], w_ref[...], preferred_element_type=F32).astype(BF16)
        kept_ref[...] = y[: total // 2]
        sent_ref[...] = y[total // 2 :]

    half = jax.ShapeDtypeStruct((total // 2, width), BF16)

    def whole(*shape):
        return pl.BlockSpec(shape, lambda j, c: (0,) * len(shape))

    return pl.pallas_call(
        kernel,
        grid_spec=pltpu.PrefetchScalarGridSpec(
            num_scalar_prefetch=1,
            grid=(width // tile,),
            in_specs=[whole(count, units)] * parts
            + [whole(1, count)] * parts
            + [whole(rank, total), whole(reqs * rank, units), pl.BlockSpec((units, tile), lambda j, c: (0, j))],
            out_specs=[whole(total, units)]
            + [pl.BlockSpec((total // 2, tile), lambda j, c: (0, j))] * 2,
            scratch_shapes=[pltpu.VMEM((total, units), F32)],
        ),
        out_shape=[jax.ShapeDtypeStruct((total, units), BF16), half, half],
        cost_estimate=SMALL,
        compiler_params=params(),
        name="feedfwd_out_first",
    )(control, *accs, *segments, lowrank, up_flat, weight)


def pick(held_at, *banks):
    reqs = held_at.shape[0]
    slots, rank = banks[0][0].shape[:2]
    count = len(banks[0])

    def kernel(at_ref, *refs):
        parts = [refs[i * count : (i + 1) * count] for i in range(len(banks))]
        outs = refs[len(banks) * count : -1]
        sems = refs[-1]

        def fetch(i, part, r):
            to = outs[i].at[r * rank : (r + 1) * rank, :]
            return pltpu.make_async_copy(part.at[lax.rem(at_ref[r], slots)], to, sems.at[i, r])

        for r in range(reqs):
            for p in range(count):

                @pl.when(at_ref[r] // slots == p)
                def _():
                    for i in range(len(banks)):
                        fetch(i, parts[i][p], r).start()

        for r in range(reqs):
            for i in range(len(banks)):
                fetch(i, parts[i][0], r).wait()

    return pl.pallas_call(
        kernel,
        grid_spec=pltpu.PrefetchScalarGridSpec(
            num_scalar_prefetch=1,
            grid=(1,),
            in_specs=[pl.BlockSpec(memory_space=pl.ANY)] * (len(banks) * count),
            out_specs=[pl.BlockSpec(memory_space=pl.ANY)] * len(banks),
            scratch_shapes=[pltpu.SemaphoreType.DMA((len(banks), reqs))],
        ),
        out_shape=[jax.ShapeDtypeStruct((reqs * rank, b[0].shape[2]), BF16) for b in banks],
        cost_estimate=SIDE,
        compiler_params=params(16),
        name="pick",
    )(held_at, *(part for bank in banks for part in bank))


def join(arrays, groups):
    rows, width = arrays[0].shape
    depth = width // groups

    per = 4
    steps = groups // per

    def kernel(*refs):
        out_ref = refs[-1]
        for i, ref in enumerate(refs[:-1]):
            for g in range(per):
                out_ref[g, :, i * depth : (i + 1) * depth] = ref[:, g * depth : (g + 1) * depth]

    return pl.pallas_call(
        kernel,
        grid=(steps,),
        in_specs=[pl.BlockSpec((rows, per * depth), lambda g: (0, g))] * len(arrays),
        out_specs=pl.BlockSpec((per, rows, len(arrays) * depth), lambda g: (g, 0, 0)),
        out_shape=jax.ShapeDtypeStruct((groups, rows, len(arrays) * depth), BF16),
        cost_estimate=SMALL,
        compiler_params=params(60),
        name="join",
    )(*arrays)


def attend(control, joined, segment, count, weight):
    total = joined.shape[0]
    depth = joined.shape[1] // 3
    rows = total // count
    first = rows // 2
    width = weight.shape[1]
    tile = width // 4

    def kernel(control_ref, joined_ref, col_ref, row_ref, w_ref, att_ref, kept_ref, sent_ref, x_scratch):
        @pl.when(pl.program_id(0) == 0)
        def _():
            across = lax.broadcasted_iota(jnp.int32, (total, total), 1)
            down = lax.broadcasted_iota(jnp.int32, (total, total), 0)
            allowed = (col_ref[...] == row_ref[...]) & (across <= down)
            for head in range(depth // HS):
                q, k, v = (
                    joined_ref[:, i * depth + head * HS : i * depth + (head + 1) * HS] for i in range(3)
                )
                scores = lax.dot_general(
                    q, k, (((1,), (1,)), ((), ())), preferred_element_type=F32
                ) * (HS ** (-0.5))
                masked = jnp.where(allowed, scores, -1e30)
                exponent = jnp.exp(masked - jnp.max(masked, axis=1, keepdims=True))
                weights = (exponent / jnp.sum(exponent, axis=1, keepdims=True)).astype(BF16)
                mixed = jnp.dot(weights, v, preferred_element_type=F32).astype(BF16)
                att_ref[:, :, head * HS : (head + 1) * HS] = mixed.reshape(count, rows, HS)
            for i in range(count):
                x_scratch[i * first : (i + 1) * first, :] = att_ref[control_ref[ORDER + i], :first, :]

        y = jnp.dot(x_scratch[...], w_ref[...], preferred_element_type=F32).astype(BF16)
        kept_ref[...] = y[: total // 4]
        sent_ref[...] = y[total // 4 :]

    half = jax.ShapeDtypeStruct((total // 4, width), BF16)
    return pl.pallas_call(
        kernel,
        grid_spec=pltpu.PrefetchScalarGridSpec(
            num_scalar_prefetch=1,
            grid=(width // tile,),
            in_specs=[
                pl.BlockSpec((total, 3 * depth), lambda j, o: (0, 0)),
                pl.BlockSpec((total, 1), lambda j, o: (0, 0)),
                pl.BlockSpec((1, total), lambda j, o: (0, 0)),
                pl.BlockSpec((depth, tile), lambda j, o: (0, j)),
            ],
            out_specs=[pl.BlockSpec((count, rows, depth), lambda j, o: (0, 0, 0))]
            + [pl.BlockSpec((total // 4, tile), lambda j, o: (0, j))] * 2,
            scratch_shapes=[pltpu.VMEM((total // 2, depth), BF16)],
        ),
        out_shape=[jax.ShapeDtypeStruct((count, rows, depth), BF16), half, half],
        cost_estimate=SMALL,
        compiler_params=params(48),
        name="attend",
    )(control, joined, segment.reshape(total, 1), segment.reshape(1, total), weight)


def write_pages(joined, lookup, key_cache, value_cache):
    pages, page, depth = key_cache.shape
    blocks = lookup.shape[0]
    hits = lookup[None, :] == jnp.arange(pages, dtype=jnp.int32)[:, None]
    source = jnp.sum(jnp.where(hits, jnp.arange(1, blocks + 1, dtype=jnp.int32)[None, :], 0), axis=1) - 1

    def kernel(source_ref, k_ref, v_ref, key_cache_ref, value_cache_ref, key_ref, value_ref):
        fresh = source_ref[pl.program_id(0)] >= 0

        @pl.when(fresh)
        def _():
            key_ref[0] = k_ref[...]
            value_ref[0] = v_ref[...]

        @pl.when(jnp.logical_not(fresh))
        def _():
            key_ref[...] = key_cache_ref[...]
            value_ref[...] = value_cache_ref[...]

    def block(part):
        return pl.BlockSpec((page, depth), lambda p, source: (jnp.maximum(source[p], 0), part))

    paged = pl.BlockSpec((1, page, depth), lambda p, source: (p, 0, 0))
    return pl.pallas_call(
        kernel,
        grid_spec=pltpu.PrefetchScalarGridSpec(
            num_scalar_prefetch=1,
            grid=(pages,),
            in_specs=[block(1), block(2), paged, paged],
            out_specs=[paged, paged],
        ),
        out_shape=[jax.ShapeDtypeStruct(key_cache.shape, BF16)] * 2,
        cost_estimate=SIDE,
        compiler_params=params(16),
        name="write_pages",
    )(source, joined, joined, key_cache, value_cache)


def shards(
    queries,
    keys,
    values,
    block_hidden_input,
    attention_out_weight,
    feedfwd_in_weight,
    feedfwd_out_weight,
    norm_gain_vector,
    norm_bias_vector,
    adapter_down_factors,
    adapter_up_factors,
    paged_key_cache,
    paged_value_cache,
    request_prompt_length,
    group_page_lookup,
    adapter_per_request,
    adapter_bank_slot,
):
    tok_rows, width = block_hidden_input.shape
    groups = lax.axis_size("mlp")
    group_rows = tok_rows * groups
    head_cols = attention_out_weight.shape[0]
    me = lax.axis_index("mlp")
    bits = [1 << i for i in range(groups.bit_length() - 1)]
    minor = len(bits) - 2
    orders = bits, bits[minor : minor + 1] + bits[:minor] + bits[minor + 1 :]
    steps = list(zip(*orders))
    width_dev = width // groups
    span = width_dev
    while span % 128:
        span *= 2
    first_core = lax.rem(lax.axis_index("req"), 2) == 0
    offsets = [jnp.asarray(block_offsets(masks), jnp.int32) for masks in orders]
    control = jnp.concatenate(
        [jnp.reshape(me * width_dev // span, (1,)), jnp.where(first_core, *offsets) ^ me]
    ).astype(jnp.int32)

    req_masks = [1 << i for i in range(lax.axis_size("req").bit_length() - 1)]
    banks = jnp.swapaxes(adapter_down_factors, 1, 2), adapter_up_factors
    banks = [[x, exchange(x, "req", req_masks[-1])] for x in banks]
    slots = adapter_down_factors.shape[0]
    adapter_ids = adapter_per_request[0]
    matched = (
        adapter_ids[:, None] == jnp.arange(adapter_bank_slot.shape[0], dtype=jnp.int32)[None, :]
    )
    wanted = jnp.sum(jnp.where(matched, adapter_bank_slot[None, :], 0), axis=1)
    part_owner = jnp.asarray(block_offsets(req_masks), jnp.int32) ^ lax.axis_index("req")
    held_slot = (
        part_owner[:, None] * slots + jnp.arange(slots, dtype=jnp.int32)[None, :]
    ).reshape(-1)
    hit = wanted[:, None] == held_slot[None, :]
    held_at = jnp.sum(jnp.where(hit, jnp.arange(hit.shape[1], dtype=jnp.int32)[None, :], 0), axis=1)

    joined = lax.all_to_all(
        join((queries, keys, values), groups), "mlp", split_axis=0, concat_axis=0, tiled=True
    ).reshape(group_rows, 3 * head_cols)

    request_ends = jnp.cumsum(request_prompt_length[0])
    positions = jnp.arange(group_rows, dtype=jnp.int32)
    segment = jnp.sum((positions[:, None] >= request_ends[None, :]).astype(jnp.int32), axis=1)
    joined, segment, control, held_at = tied(joined, segment, control, held_at)
    attended, *partial_a = attend(control, joined, segment, groups, attention_out_weight)
    partial_b = out_projection(control, attended, 1, attention_out_weight)
    kept_a, sent_a = reduce_step(*partial_a, steps[0])
    sent_a = after(sent_a, partial_b)

    sent_a, joined, banks = tied(sent_a, joined, banks)
    for mask in req_masks[-2::-1]:
        banks = [parts + [exchange(part, "req", mask) for part in parts] for parts in banks]
    pages_out = write_pages(joined, group_page_lookup[0], paged_key_cache, paged_value_cache)
    factors = pick(held_at, *banks)

    vectors = norm_gain_vector, norm_bias_vector
    sum_a = reduce_rows(kept_a, sent_a, steps[1:])
    partial_b = reduce_step(*partial_b, steps[0])
    sum_a = after(sum_a, partial_b)
    residual_a, rows_a = norm(block_hidden_input, 0, sum_a, *vectors)
    for masks in steps[1:-1]:
        partial_b = reduce_step(*partial_b, masks)
    rows_a = grow(rows_a, steps[-1], partial_b)
    sum_b, (key_pages_out, value_pages_out), (down_flat, up_flat), _ = tied(
        reduce_rows(*partial_b, steps[-1:]), pages_out, factors, rows_a
    )
    residual_b, rows_b = norm(block_hidden_input, 1, sum_b, *vectors)
    ahead = steps[-2::-1]
    for masks, masks_ahead in zip(steps[:0:-1], ahead):
        if masks_ahead is steps[0]:
            rows_a = rows_a, swap(rows_a, masks_ahead)
            rows_b = grow(rows_b, masks, rows_a[1])
        else:
            rows_a = grow(rows_a, masks_ahead)
            rows_b = grow(rows_b, masks, rows_a)
    rows_b = rows_b, swap(rows_b, steps[0])

    part_rows = tok_rows // 2
    segments = [
        segment.reshape(groups, 2, part_rows)[:, part].reshape(1, groups * part_rows)
        for part in range(2)
    ]
    win = feedfwd_in_weight.T
    low_a = down_products(control, *rows_a, groups, down_flat, segments[0])
    acc_a = feedfwd_in([rows_a], win, 0)
    rows_b, low_a, acc_a = tied(rows_b, low_a, acc_a)
    low_b = down_products(control, *rows_b, groups, down_flat, segments[1])
    lowrank = jnp.concatenate([low_a, low_b], axis=1)
    acc_b = feedfwd_in([rows_b], win, 0)
    for mask in bits[:minor]:
        lowrank = lowrank + exchange(lowrank, "mlp", mask)
    lowrank, acc_b = tied(lowrank, acc_b)
    lowrank = lowrank + sum(
        exchange(lowrank, "mlp", k << minor) for k in range(1, groups >> minor)
    )
    acc = feedfwd_in([rows_a, rows_b], win, 1, acc_a + acc_b)

    wide = width * 3 // 5
    tile = wide // 3
    activated, *partial_a = feedfwd_out_first(
        control, acc, lowrank, segments, up_flat, feedfwd_out_weight, wide, tile, groups
    )
    partial_b = feedfwd_out(activated, feedfwd_out_weight, wide, width - wide, tile)
    partial_a = reduce_step(*partial_a, steps[0])
    partial_a, partial_b = tied(partial_a, partial_b)
    partial_b = reduce_step(*partial_b, steps[0])
    for masks in steps[1:-1]:
        partial_a = reduce_step(*partial_a, masks)
        partial_a, partial_b = tied(partial_a, partial_b)
        partial_b = reduce_step(*partial_b, masks)
    sums = (
        (partial_a[0], swap(partial_a[1], steps[-1])),
        (partial_b[0], swap(partial_b[1], steps[-1])),
    )
    block_out = (
        jnp.concatenate([residual_a, residual_b], axis=0)
        + jnp.concatenate([a.astype(F32) + b.astype(F32) for a, b in sums], axis=1)
    ).astype(BF16)
    return (block_out, key_pages_out, value_pages_out)


def solution(mesh):
    in_specs = (
        P(("req", "mlp"), None),
        P(("req", "mlp"), None),
        P(("req", "mlp"), None),
        P(("req", "mlp"), None),
        P("mlp", None),
        P(None, "mlp"),
        P("mlp", None),
        P(),
        P(),
        P("req", "mlp", None),
        P("req", None, "mlp"),
        P("req", None, "mlp"),
        P("req", None, "mlp"),
        P("req", None),
        P("req", None),
        P("req", None),
        P(),
    )
    out_specs = (P(("req", "mlp"), None), P("req", None, "mlp"), P("req", None, "mlp"))
    return jax.shard_map(shards, mesh=mesh, in_specs=in_specs, out_specs=out_specs, check_vma=False)
```

```python
import functools

import jax
import jax.numpy as jnp
from jax import lax
from jax.experimental import pallas as pl
from jax.experimental.pallas import tpu as pltpu
from jax.sharding import PartitionSpec as P

HS = 128
ADAPTER_RANK = 16
REQS = 16
PAGE = 128
EPS = 1e-06
MIB = 1024 * 1024
SPAN, ORDER = range(2)
BF16 = jnp.bfloat16
F32 = jnp.float32


def params(mib=22):
    return pltpu.CompilerParams(vmem_limit_bytes=mib * MIB)


SMALL = pl.CostEstimate(flops=0, bytes_accessed=1, transcendentals=0)
SIDE = pl.CostEstimate(flops=0, bytes_accessed=8 * MIB, transcendentals=0)


def exchange(x, axis, mask):
    size = lax.axis_size(axis)
    return lax.ppermute(x, axis, [(i, i ^ mask) for i in range(size)])


def swap(x, masks):
    reqs, size = lax.axis_size("req"), lax.axis_size("mlp")
    pairs = [
        (r * size + i, r * size + (i ^ masks[r % 2])) for r in range(reqs) for i in range(size)
    ]
    return lax.ppermute(x, ("req", "mlp"), pairs)


def block_offsets(masks):
    offsets = [0]
    for mask in reversed(masks):
        offsets = offsets + [o ^ mask for o in offsets]
    return offsets


def reduce_step(kept, sent, masks):
    rows, width = kept.shape
    half = rows // 2

    def kernel(kept_ref, got_ref, out_ref, next_ref):
        out_ref[...] = kept_ref[:half].astype(F32) + got_ref[:half].astype(F32)
        next_ref[...] = (kept_ref[half:].astype(F32) + got_ref[half:].astype(F32)).astype(BF16)

    return pl.pallas_call(
        kernel,
        out_shape=[jax.ShapeDtypeStruct((half, width), t) for t in (F32, BF16)],
        cost_estimate=SMALL,
        compiler_params=params(16),
        name="reduce_step",
    )(kept, swap(sent, masks))


def reduce_rows(kept, sent, steps):
    for masks in steps[:-1]:
        kept, sent = reduce_step(kept, sent, masks)
    return kept, swap(sent, steps[-1])


def grow(rows, masks, *first):
    return jnp.concatenate([rows, after(swap(rows, masks), *first)], axis=0)


def tied(*values):
    return lax.optimization_barrier(values)


def after(value, *first):
    return tied(value, *first)[0]


def out_projection(control, blocks, part, weight):
    count, rows, depth = blocks.shape
    rows = rows // 2
    total = count * rows
    width = weight.shape[1]
    tile = width // 4

    def kernel(control_ref, x_ref, w_ref, kept_ref, sent_ref, x_scratch):
        @pl.when(pl.program_id(0) == 0)
        def _():
            for i in range(count):
                x = x_ref[control_ref[ORDER + i], part * rows : (part + 1) * rows, :]
                x_scratch[i * rows : (i + 1) * rows, :] = x

        y = jnp.dot(x_scratch[...], w_ref[...], preferred_element_type=F32).astype(BF16)
        kept_ref[...] = y[: total // 2]
        sent_ref[...] = y[total // 2 :]

    half = jax.ShapeDtypeStruct((total // 2, width), BF16)
    return pl.pallas_call(
        kernel,
        grid_spec=pltpu.PrefetchScalarGridSpec(
            num_scalar_prefetch=1,
            grid=(width // tile,),
            in_specs=[
                pl.BlockSpec(blocks.shape, lambda j, c: (0, 0, 0)),
                pl.BlockSpec((depth, tile), lambda j, c: (0, j)),
            ],
            out_specs=[pl.BlockSpec((total // 2, tile), lambda j, c: (0, j))] * 2,
            scratch_shapes=[pltpu.VMEM((total, depth), BF16)],
        ),
        out_shape=[half, half],
        cost_estimate=SMALL,
        compiler_params=params(48),
        name="out_projection",
    )(control, blocks, weight)


def feedfwd_out(activated, weight, start, width, tile):
    total, depth = activated.shape
    first = start // tile

    def kernel(x_ref, w_ref, kept_ref, sent_ref):
        y = jnp.dot(x_ref[...], w_ref[...], preferred_element_type=F32).astype(BF16)
        kept_ref[...] = y[: total // 2]
        sent_ref[...] = y[total // 2 :]

    half = jax.ShapeDtypeStruct((total // 2, width), BF16)
    return pl.pallas_call(
        kernel,
        grid=(width // tile,),
        in_specs=[
            pl.BlockSpec((total, depth), lambda j: (0, 0)),
            pl.BlockSpec((depth, tile), lambda j: (0, first + j)),
        ],
        out_specs=[pl.BlockSpec((total // 2, tile), lambda j: (0, j))] * 2,
        out_shape=[half, half],
        cost_estimate=SMALL,
        compiler_params=params(),
        name="feedfwd_out",
    )(activated, weight)


def norm(hidden, part, sums, gain, bias):
    width = hidden.shape[1]
    rows = hidden.shape[0] // 2

    def kernel(hidden_ref, a_ref, b_ref, gain_ref, bias_ref, residual_ref, out_ref):
        residual = hidden_ref[part * rows : (part + 1) * rows, :].astype(F32) + (
            a_ref[...].astype(F32) + b_ref[...].astype(F32)
        )
        residual_ref[...] = residual
        centered = residual - jnp.sum(residual, axis=1, keepdims=True) * (1.0 / width)
        var = jnp.sum(centered * centered, axis=1, keepdims=True) * (1.0 / width)
        out_ref[...] = (centered * lax.rsqrt(var + EPS) * gain_ref[...] + bias_ref[...]).astype(BF16)

    return pl.pallas_call(
        kernel,
        out_shape=[jax.ShapeDtypeStruct((rows, width), t) for t in (F32, BF16)],
        cost_estimate=SMALL,
        compiler_params=params(16),
        name="norm",
    )(hidden, *sums, gain.reshape(1, width), bias.reshape(1, width))


def streamed(weight):
    return pltpu.with_memory_space_constraint(weight, pltpu.HBM)


def feedfwd_in(parts, weight, which, accs=()):
    half, width = parts[0][0].shape
    units = weight.shape[0]
    count = len(parts)
    steps = 2
    piece = width // (2 * steps)

    def kernel(*refs):
        rows, w_ref = refs[: 2 * count], refs[2 * count]
        acc_refs, outs = refs[2 * count + 1 : -count], refs[-count:]
        x = jnp.concatenate([ref[...] for ref in rows], axis=0)
        y = lax.dot_general(x, w_ref[...], (((1,), (1,)), ((), ())), preferred_element_type=F32)

        @pl.when(pl.program_id(0) == 0)
        def _():
            for i, out_ref in enumerate(outs):
                here = y[2 * half * i : 2 * half * (i + 1)]
                out_ref[...] = acc_refs[i][...] + here if acc_refs else here

        @pl.when(pl.program_id(0) > 0)
        def _():
            for i, out_ref in enumerate(outs):
                out_ref[...] += y[2 * half * i : 2 * half * (i + 1)]

    rows = pl.BlockSpec((half, piece), lambda k: (0, which * steps + k))
    full = pl.BlockSpec((2 * half, units), lambda k: (0, 0))
    return pl.pallas_call(
        kernel,
        grid=(steps,),
        in_specs=[rows] * (2 * count)
        + [pl.BlockSpec((units, piece), lambda k: (0, which * steps + k))]
        + [full] * len(accs),
        out_specs=[full] * count,
        out_shape=[jax.ShapeDtypeStruct((2 * half, units), F32)] * count,
        cost_estimate=pl.CostEstimate(
            flops=4 * count * steps * half * piece * units,
            bytes_accessed=2 * steps * piece * units,
            transcendentals=0,
        ),
        compiler_params=params(24),
        name="feedfwd_in",
    )(*(x for part in parts for x in part), streamed(weight), *accs)


def down_products(control, upper, lower, groups, down_flat, segment):
    half = upper.shape[0]
    total = 2 * half
    rows = total // groups
    per = groups // 2
    width = down_flat.shape[1]
    reps = 1
    while (reps * width) % 128:
        reps *= 2
    span = reps * width
    if reps > 1:
        pos = lax.rem(lax.axis_index("mlp"), reps)
        down_flat = jnp.concatenate(
            [jnp.where(pos == i, down_flat, jnp.zeros_like(down_flat)) for i in range(reps)], axis=1
        )
    reqs = REQS
    rank = down_flat.shape[0] // reqs

    def kernel(control_ref, a_ref, b_ref, down_ref, segment_ref, out_ref, x_scratch):
        for i in range(groups):
            start = pl.multiple_of(control_ref[ORDER + i] * rows, rows)
            x = (a_ref if i < per else b_ref)[(i % per) * rows : (i % per + 1) * rows, :]
            x_scratch[pl.ds(start, rows), :] = x

        every_rank = lax.dot_general(
            down_ref[...], x_scratch[...], (((1,), (1,)), ((), ())), preferred_element_type=F32
        ).reshape(reqs, rank, total)
        chosen = lax.broadcasted_iota(jnp.int32, (reqs, total), 0) == segment_ref[...]
        out_ref[...] = jnp.sum(jnp.where(chosen[:, None, :], every_rank, 0.0), axis=0)

    own = pl.BlockSpec((half, span), lambda k, c: (0, c[SPAN]))
    return pl.pallas_call(
        kernel,
        grid_spec=pltpu.PrefetchScalarGridSpec(
            num_scalar_prefetch=1,
            grid=(1,),
            in_specs=[own, own]
            + [pl.BlockSpec(x.shape, lambda k, c: (0, 0)) for x in (down_flat, segment)],
            out_specs=pl.BlockSpec((rank, total), lambda k, c: (0, 0)),
            scratch_shapes=[pltpu.VMEM((total, span), BF16)],
        ),
        out_shape=jax.ShapeDtypeStruct((rank, total), F32),
        cost_estimate=SMALL,
        compiler_params=params(16),
        name="down_products",
    )(control, upper, lower, down_flat, segment)


def feedfwd_out_first(control, accs, lowrank, segments, up_flat, weight, width, tile, groups):
    count, units = accs[0].shape
    parts = len(accs)
    total = parts * count
    reqs, rank = REQS, lowrank.shape[0]
    rows = count // groups

    def kernel(control_ref, *refs):
        acc_refs, segment_refs = (refs[i * parts : (i + 1) * parts] for i in range(2))
        low_ref, up_ref, w_ref, act_ref, kept_ref, sent_ref, up_scratch = refs[2 * parts :]

        @pl.when(pl.program_id(0) == 0)
        def _():
            spreads = []
            for part, segment_ref in enumerate(segment_refs):
                low = low_ref[:, part * count : (part + 1) * count].astype(BF16).astype(F32)
                chosen = lax.broadcasted_iota(jnp.int32, (reqs, count), 0) == segment_ref[...]
                spread = jnp.where(chosen[:, None, :], low[None, :, :], 0.0)
                spreads.append(spread.reshape(reqs * rank, count).astype(BF16))
            up_scratch[...] = lax.dot_general(
                jnp.concatenate(spreads, axis=1),
                up_ref[...],
                (((0,), (0,)), ((), ())),
                preferred_element_type=F32,
            )
            for i in range(groups):
                for part, acc_ref in enumerate(acc_refs):
                    start = pl.multiple_of(part * count + control_ref[ORDER + i] * rows, rows)
                    preact = acc_ref[i * rows : (i + 1) * rows, :] + up_scratch[pl.ds(start, rows), :]
                    here = (i * parts + part) * rows
                    act_ref[here : here + rows, :] = jax.nn.gelu(preact, approximate=True).astype(BF16)

        y = jnp.dot(act_ref[...], w_ref[...], preferred_element_type=F32).astype(BF16)
        kept_ref[...] = y[: total // 2]
        sent_ref[...] = y[total // 2 :]

    half = jax.ShapeDtypeStruct((total // 2, width), BF16)

    def whole(*shape):
        return pl.BlockSpec(shape, lambda j, c: (0,) * len(shape))

    return pl.pallas_call(
        kernel,
        grid_spec=pltpu.PrefetchScalarGridSpec(
            num_scalar_prefetch=1,
            grid=(width // tile,),
            in_specs=[whole(count, units)] * parts
            + [whole(1, count)] * parts
            + [whole(rank, total), whole(reqs * rank, units), pl.BlockSpec((units, tile), lambda j, c: (0, j))],
            out_specs=[whole(total, units)]
            + [pl.BlockSpec((total // 2, tile), lambda j, c: (0, j))] * 2,
            scratch_shapes=[pltpu.VMEM((total, units), F32)],
        ),
        out_shape=[jax.ShapeDtypeStruct((total, units), BF16), half, half],
        cost_estimate=SMALL,
        compiler_params=params(),
        name="feedfwd_out_first",
    )(control, *accs, *segments, lowrank, up_flat, weight)


def pick(held_at, *banks):
    reqs = held_at.shape[0]
    slots, rank = banks[0][0].shape[:2]
    count = len(banks[0])

    def kernel(at_ref, *refs):
        parts = [refs[i * count : (i + 1) * count] for i in range(len(banks))]
        outs = refs[len(banks) * count : -1]
        sems = refs[-1]

        def fetch(i, part, r):
            to = outs[i].at[r * rank : (r + 1) * rank, :]
            return pltpu.make_async_copy(part.at[lax.rem(at_ref[r], slots)], to, sems.at[i, r])

        for r in range(reqs):
            for p in range(count):

                @pl.when(at_ref[r] // slots == p)
                def _():
                    for i in range(len(banks)):
                        fetch(i, parts[i][p], r).start()

        for r in range(reqs):
            for i in range(len(banks)):
                fetch(i, parts[i][0], r).wait()

    return pl.pallas_call(
        kernel,
        grid_spec=pltpu.PrefetchScalarGridSpec(
            num_scalar_prefetch=1,
            grid=(1,),
            in_specs=[pl.BlockSpec(memory_space=pl.ANY)] * (len(banks) * count),
            out_specs=[pl.BlockSpec(memory_space=pl.ANY)] * len(banks),
            scratch_shapes=[pltpu.SemaphoreType.DMA((len(banks), reqs))],
        ),
        out_shape=[jax.ShapeDtypeStruct((reqs * rank, b[0].shape[2]), BF16) for b in banks],
        cost_estimate=SIDE,
        compiler_params=params(16),
        name="pick",
    )(held_at, *(part for bank in banks for part in bank))


def join(arrays, groups):
    rows, width = arrays[0].shape
    depth = width // groups

    per = 4
    steps = groups // per

    def kernel(*refs):
        out_ref = refs[-1]
        for i, ref in enumerate(refs[:-1]):
            for g in range(per):
                out_ref[g, :, i * depth : (i + 1) * depth] = ref[:, g * depth : (g + 1) * depth]

    return pl.pallas_call(
        kernel,
        grid=(steps,),
        in_specs=[pl.BlockSpec((rows, per * depth), lambda g: (0, g))] * len(arrays),
        out_specs=pl.BlockSpec((per, rows, len(arrays) * depth), lambda g: (g, 0, 0)),
        out_shape=jax.ShapeDtypeStruct((groups, rows, len(arrays) * depth), BF16),
        cost_estimate=SMALL,
        compiler_params=params(60),
        name="join",
    )(*arrays)


def attend(control, joined, segment, count, weight):
    total = joined.shape[0]
    depth = joined.shape[1] // 3
    rows = total // count
    first = rows // 2
    width = weight.shape[1]
    tile = width // 4

    def kernel(control_ref, joined_ref, col_ref, row_ref, w_ref, att_ref, kept_ref, sent_ref, x_scratch):
        @pl.when(pl.program_id(0) == 0)
        def _():
            across = lax.broadcasted_iota(jnp.int32, (total, total), 1)
            down = lax.broadcasted_iota(jnp.int32, (total, total), 0)
            allowed = (col_ref[...] == row_ref[...]) & (across <= down)
            for head in range(depth // HS):
                q, k, v = (
                    joined_ref[:, i * depth + head * HS : i * depth + (head + 1) * HS] for i in range(3)
                )
                scores = lax.dot_general(
                    q, k, (((1,), (1,)), ((), ())), preferred_element_type=F32
                ) * (HS ** (-0.5))
                masked = jnp.where(allowed, scores, -1e30)
                exponent = jnp.exp(masked - jnp.max(masked, axis=1, keepdims=True))
                weights = (exponent / jnp.sum(exponent, axis=1, keepdims=True)).astype(BF16)
                mixed = jnp.dot(weights, v, preferred_element_type=F32).astype(BF16)
                att_ref[:, :, head * HS : (head + 1) * HS] = mixed.reshape(count, rows, HS)
            for i in range(count):
                x_scratch[i * first : (i + 1) * first, :] = att_ref[control_ref[ORDER + i], :first, :]

        y = jnp.dot(x_scratch[...], w_ref[...], preferred_element_type=F32).astype(BF16)
        kept_ref[...] = y[: total // 4]
        sent_ref[...] = y[total // 4 :]

    half = jax.ShapeDtypeStruct((total // 4, width), BF16)
    return pl.pallas_call(
        kernel,
        grid_spec=pltpu.PrefetchScalarGridSpec(
            num_scalar_prefetch=1,
            grid=(width // tile,),
            in_specs=[
                pl.BlockSpec((total, 3 * depth), lambda j, o: (0, 0)),
                pl.BlockSpec((total, 1), lambda j, o: (0, 0)),
                pl.BlockSpec((1, total), lambda j, o: (0, 0)),
                pl.BlockSpec((depth, tile), lambda j, o: (0, j)),
            ],
            out_specs=[pl.BlockSpec((count, rows, depth), lambda j, o: (0, 0, 0))]
            + [pl.BlockSpec((total // 4, tile), lambda j, o: (0, j))] * 2,
            scratch_shapes=[pltpu.VMEM((total // 2, depth), BF16)],
        ),
        out_shape=[jax.ShapeDtypeStruct((count, rows, depth), BF16), half, half],
        cost_estimate=SMALL,
        compiler_params=params(48),
        name="attend",
    )(control, joined, segment.reshape(total, 1), segment.reshape(1, total), weight)


def write_pages(joined, lookup, key_cache, value_cache):
    pages, page, depth = key_cache.shape
    blocks = lookup.shape[0]
    hits = lookup[None, :] == jnp.arange(pages, dtype=jnp.int32)[:, None]
    source = jnp.sum(jnp.where(hits, jnp.arange(1, blocks + 1, dtype=jnp.int32)[None, :], 0), axis=1) - 1

    def kernel(source_ref, k_ref, v_ref, key_cache_ref, value_cache_ref, key_ref, value_ref):
        fresh = source_ref[pl.program_id(0)] >= 0

        @pl.when(fresh)
        def _():
            key_ref[0] = k_ref[...]
            value_ref[0] = v_ref[...]

        @pl.when(jnp.logical_not(fresh))
        def _():
            key_ref[...] = key_cache_ref[...]
            value_ref[...] = value_cache_ref[...]

    def block(part):
        return pl.BlockSpec((page, depth), lambda p, source: (jnp.maximum(source[p], 0), part))

    paged = pl.BlockSpec((1, page, depth), lambda p, source: (p, 0, 0))
    return pl.pallas_call(
        kernel,
        grid_spec=pltpu.PrefetchScalarGridSpec(
            num_scalar_prefetch=1,
            grid=(pages,),
            in_specs=[block(1), block(2), paged, paged],
            out_specs=[paged, paged],
        ),
        out_shape=[jax.ShapeDtypeStruct(key_cache.shape, BF16)] * 2,
        cost_estimate=SIDE,
        compiler_params=params(16),
        name="write_pages",
    )(source, joined, joined, key_cache, value_cache)


def shards(
    queries,
    keys,
    values,
    block_hidden_input,
    attention_out_weight,
    feedfwd_in_weight,
    feedfwd_out_weight,
    norm_gain_vector,
    norm_bias_vector,
    adapter_down_factors,
    adapter_up_factors,
    paged_key_cache,
    paged_value_cache,
    request_prompt_length,
    group_page_lookup,
    adapter_per_request,
    adapter_bank_slot,
):
    tok_rows, width = block_hidden_input.shape
    groups = lax.axis_size("mlp")
    group_rows = tok_rows * groups
    head_cols = attention_out_weight.shape[0]
    me = lax.axis_index("mlp")
    bits = [1 << i for i in range(groups.bit_length() - 1)]
    minor = len(bits) - 2
    orders = bits, bits[minor : minor + 1] + bits[:minor] + bits[minor + 1 :]
    steps = list(zip(*orders))
    width_dev = width // groups
    span = width_dev
    while span % 128:
        span *= 2
    first_core = lax.rem(lax.axis_index("req"), 2) == 0
    offsets = [jnp.asarray(block_offsets(masks), jnp.int32) for masks in orders]
    control = jnp.concatenate(
        [jnp.reshape(me * width_dev // span, (1,)), jnp.where(first_core, *offsets) ^ me]
    ).astype(jnp.int32)

    req_masks = [1 << i for i in range(lax.axis_size("req").bit_length() - 1)]
    banks = jnp.swapaxes(adapter_down_factors, 1, 2), adapter_up_factors
    banks = [[x, exchange(x, "req", req_masks[-1])] for x in banks]
    slots = adapter_down_factors.shape[0]
    adapter_ids = adapter_per_request[0]
    matched = (
        adapter_ids[:, None] == jnp.arange(adapter_bank_slot.shape[0], dtype=jnp.int32)[None, :]
    )
    wanted = jnp.sum(jnp.where(matched, adapter_bank_slot[None, :], 0), axis=1)
    part_owner = jnp.asarray(block_offsets(req_masks), jnp.int32) ^ lax.axis_index("req")
    held_slot = (
        part_owner[:, None] * slots + jnp.arange(slots, dtype=jnp.int32)[None, :]
    ).reshape(-1)
    hit = wanted[:, None] == held_slot[None, :]
    held_at = jnp.sum(jnp.where(hit, jnp.arange(hit.shape[1], dtype=jnp.int32)[None, :], 0), axis=1)

    joined = lax.all_to_all(
        join((queries, keys, values), groups), "mlp", split_axis=0, concat_axis=0, tiled=True
    ).reshape(group_rows, 3 * head_cols)

    request_ends = jnp.cumsum(request_prompt_length[0])
    positions = jnp.arange(group_rows, dtype=jnp.int32)
    segment = jnp.sum((positions[:, None] >= request_ends[None, :]).astype(jnp.int32), axis=1)
    joined, segment, control, held_at = tied(joined, segment, control, held_at)
    attended, *partial_a = attend(control, joined, segment, groups, attention_out_weight)
    partial_b = out_projection(control, attended, 1, attention_out_weight)
    kept_a, sent_a = reduce_step(*partial_a, steps[0])
    sent_a = after(sent_a, partial_b)

    sent_a, joined, banks = tied(sent_a, joined, banks)
    for mask in req_masks[-2::-1]:
        banks = [parts + [exchange(part, "req", mask) for part in parts] for parts in banks]
    pages_out = write_pages(joined, group_page_lookup[0], paged_key_cache, paged_value_cache)
    factors = pick(held_at, *banks)

    vectors = norm_gain_vector, norm_bias_vector
    sum_a = reduce_rows(kept_a, sent_a, steps[1:])
    partial_b = reduce_step(*partial_b, steps[0])
    sum_a = after(sum_a, partial_b)
    residual_a, rows_a = norm(block_hidden_input, 0, sum_a, *vectors)
    for masks in steps[1:-1]:
        partial_b = reduce_step(*partial_b, masks)
    rows_a = grow(rows_a, steps[-1], partial_b)
    sum_b, (key_pages_out, value_pages_out), (down_flat, up_flat), _ = tied(
        reduce_rows(*partial_b, steps[-1:]), pages_out, factors, rows_a
    )
    residual_b, rows_b = norm(block_hidden_input, 1, sum_b, *vectors)
    ahead = steps[-2::-1]
    for masks, masks_ahead in zip(steps[:0:-1], ahead):
        if masks_ahead is steps[0]:
            rows_a = rows_a, swap(rows_a, masks_ahead)
            rows_b = grow(rows_b, masks, rows_a[1])
        else:
            rows_a = grow(rows_a, masks_ahead)
            rows_b = grow(rows_b, masks, rows_a)
    rows_b = rows_b, swap(rows_b, steps[0])

    part_rows = tok_rows // 2
    segments = [
        segment.reshape(groups, 2, part_rows)[:, part].reshape(1, groups * part_rows)
        for part in range(2)
    ]
    win = feedfwd_in_weight.T
    low_a = down_products(control, *rows_a, groups, down_flat, segments[0])
    acc_a = feedfwd_in([rows_a], win, 0)
    rows_b, low_a, acc_a = tied(rows_b, low_a, acc_a)
    low_b = down_products(control, *rows_b, groups, down_flat, segments[1])
    lowrank = jnp.concatenate([low_a, low_b], axis=1)
    acc_b = feedfwd_in([rows_b], win, 0)
    for mask in bits[:minor]:
        lowrank = lowrank + exchange(lowrank, "mlp", mask)
    lowrank, acc_b = tied(lowrank, acc_b)
    lowrank = lowrank + sum(
        exchange(lowrank, "mlp", k << minor) for k in range(1, groups >> minor)
    )
    acc = feedfwd_in([rows_a, rows_b], win, 1, acc_a + acc_b)

    wide = width // 2
    tile = wide // 2
    activated, *partial_a = feedfwd_out_first(
        control, acc, lowrank, segments, up_flat, feedfwd_out_weight, wide, tile, groups
    )
    partial_b = feedfwd_out(activated, feedfwd_out_weight, wide, width - wide, tile)
    partial_a = reduce_step(*partial_a, steps[0])
    partial_b = reduce_step(*after(partial_b, partial_a), steps[0])
    for masks in steps[1:-1]:
        partial_a = reduce_step(*partial_a, masks)
        partial_b = reduce_step(*after(partial_b, partial_a), masks)
    sums = (
        (partial_a[0], swap(partial_a[1], steps[-1])),
        (partial_b[0], swap(partial_b[1], steps[-1])),
    )
    block_out = (
        jnp.concatenate([residual_a, residual_b], axis=0)
        + jnp.concatenate([a.astype(F32) + b.astype(F32) for a, b in sums], axis=1)
    ).astype(BF16)
    return (block_out, key_pages_out, value_pages_out)


def solution(mesh):
    in_specs = (
        P(("req", "mlp"), None),
        P(("req", "mlp"), None),
        P(("req", "mlp"), None),
        P(("req", "mlp"), None),
        P("mlp", None),
        P(None, "mlp"),
        P("mlp", None),
        P(),
        P(),
        P("req", "mlp", None),
        P("req", None, "mlp"),
        P("req", None, "mlp"),
        P("req", None, "mlp"),
        P("req", None),
        P("req", None),
        P("req", None),
        P(),
    )
    out_specs = (P(("req", "mlp"), None), P("req", None, "mlp"), P("req", None, "mlp"))
    return jax.shard_map(shards, mesh=mesh, in_specs=in_specs, out_specs=out_specs, check_vma=False)
```

```python
import functools

import jax
import jax.numpy as jnp
from jax import lax
from jax.experimental import pallas as pl
from jax.experimental.pallas import tpu as pltpu
from jax.sharding import PartitionSpec as P

HS = 128
ADAPTER_RANK = 16
REQS = 16
PAGE = 128
EPS = 1e-06
MIB = 1024 * 1024
SPAN, ORDER = range(2)
BF16 = jnp.bfloat16
F32 = jnp.float32


def params(mib=22):
    return pltpu.CompilerParams(vmem_limit_bytes=mib * MIB)


SMALL = pl.CostEstimate(flops=0, bytes_accessed=1, transcendentals=0)
SIDE = pl.CostEstimate(flops=0, bytes_accessed=8 * MIB, transcendentals=0)


def exchange(x, axis, mask):
    size = lax.axis_size(axis)
    return lax.ppermute(x, axis, [(i, i ^ mask) for i in range(size)])


def swap(x, masks):
    reqs, size = lax.axis_size("req"), lax.axis_size("mlp")
    pairs = [
        (r * size + i, r * size + (i ^ masks[r % 2])) for r in range(reqs) for i in range(size)
    ]
    return lax.ppermute(x, ("req", "mlp"), pairs)


def block_offsets(masks):
    offsets = [0]
    for mask in reversed(masks):
        offsets = offsets + [o ^ mask for o in offsets]
    return offsets


def reduce_step(kept, sent, masks):
    rows, width = kept.shape
    half = rows // 2

    def kernel(kept_ref, got_ref, out_ref, next_ref):
        out_ref[...] = kept_ref[:half].astype(F32) + got_ref[:half].astype(F32)
        next_ref[...] = (kept_ref[half:].astype(F32) + got_ref[half:].astype(F32)).astype(BF16)

    return pl.pallas_call(
        kernel,
        out_shape=[jax.ShapeDtypeStruct((half, width), t) for t in (F32, BF16)],
        cost_estimate=SMALL,
        compiler_params=params(16),
        name="reduce_step",
    )(kept, swap(sent, masks))


def reduce_rows(kept, sent, steps):
    for masks in steps[:-1]:
        kept, sent = reduce_step(kept, sent, masks)
    return kept, swap(sent, steps[-1])


def grow(rows, masks, *first):
    return jnp.concatenate([rows, after(swap(rows, masks), *first)], axis=0)


def tied(*values):
    return lax.optimization_barrier(values)


def after(value, *first):
    return tied(value, *first)[0]


def out_projection(control, blocks, part, weight):
    count, rows, depth = blocks.shape
    rows = rows // 2
    total = count * rows
    width = weight.shape[1]
    tile = width // 4

    def kernel(control_ref, x_ref, w_ref, kept_ref, sent_ref, x_scratch):
        @pl.when(pl.program_id(0) == 0)
        def _():
            for i in range(count):
                x = x_ref[control_ref[ORDER + i], part * rows : (part + 1) * rows, :]
                x_scratch[i * rows : (i + 1) * rows, :] = x

        y = jnp.dot(x_scratch[...], w_ref[...], preferred_element_type=F32).astype(BF16)
        kept_ref[...] = y[: total // 2]
        sent_ref[...] = y[total // 2 :]

    half = jax.ShapeDtypeStruct((total // 2, width), BF16)
    return pl.pallas_call(
        kernel,
        grid_spec=pltpu.PrefetchScalarGridSpec(
            num_scalar_prefetch=1,
            grid=(width // tile,),
            in_specs=[
                pl.BlockSpec(blocks.shape, lambda j, c: (0, 0, 0)),
                pl.BlockSpec((depth, tile), lambda j, c: (0, j)),
            ],
            out_specs=[pl.BlockSpec((total // 2, tile), lambda j, c: (0, j))] * 2,
            scratch_shapes=[pltpu.VMEM((total, depth), BF16)],
        ),
        out_shape=[half, half],
        cost_estimate=SMALL,
        compiler_params=params(48),
        name="out_projection",
    )(control, blocks, weight)


def feedfwd_out(activated, weight, start, width, tile):
    total, depth = activated.shape
    first = start // tile

    def kernel(x_ref, w_ref, kept_ref, sent_ref):
        y = jnp.dot(x_ref[...], w_ref[...], preferred_element_type=F32).astype(BF16)
        kept_ref[...] = y[: total // 2]
        sent_ref[...] = y[total // 2 :]

    half = jax.ShapeDtypeStruct((total // 2, width), BF16)
    return pl.pallas_call(
        kernel,
        grid=(width // tile,),
        in_specs=[
            pl.BlockSpec((total, depth), lambda j: (0, 0)),
            pl.BlockSpec((depth, tile), lambda j: (0, first + j)),
        ],
        out_specs=[pl.BlockSpec((total // 2, tile), lambda j: (0, j))] * 2,
        out_shape=[half, half],
        cost_estimate=SMALL,
        compiler_params=params(),
        name="feedfwd_out",
    )(activated, weight)


def norm(hidden, part, sums, gain, bias):
    width = hidden.shape[1]
    rows = hidden.shape[0] // 2

    def kernel(hidden_ref, a_ref, b_ref, gain_ref, bias_ref, residual_ref, out_ref):
        residual = hidden_ref[part * rows : (part + 1) * rows, :].astype(F32) + (
            a_ref[...].astype(F32) + b_ref[...].astype(F32)
        )
        residual_ref[...] = residual
        centered = residual - jnp.sum(residual, axis=1, keepdims=True) * (1.0 / width)
        var = jnp.sum(centered * centered, axis=1, keepdims=True) * (1.0 / width)
        out_ref[...] = (centered * lax.rsqrt(var + EPS) * gain_ref[...] + bias_ref[...]).astype(BF16)

    return pl.pallas_call(
        kernel,
        out_shape=[jax.ShapeDtypeStruct((rows, width), t) for t in (F32, BF16)],
        cost_estimate=SMALL,
        compiler_params=params(16),
        name="norm",
    )(hidden, *sums, gain.reshape(1, width), bias.reshape(1, width))


def streamed(weight):
    return pltpu.with_memory_space_constraint(weight, pltpu.HBM)


def feedfwd_in(parts, weight, which, accs=()):
    half, width = parts[0][0].shape
    units = weight.shape[0]
    count = len(parts)
    steps = 2
    piece = width // (2 * steps)

    def kernel(*refs):
        rows, w_ref = refs[: 2 * count], refs[2 * count]
        acc_refs, outs = refs[2 * count + 1 : -count], refs[-count:]
        x = jnp.concatenate([ref[...] for ref in rows], axis=0)
        y = lax.dot_general(x, w_ref[...], (((1,), (1,)), ((), ())), preferred_element_type=F32)

        @pl.when(pl.program_id(0) == 0)
        def _():
            for i, out_ref in enumerate(outs):
                here = y[2 * half * i : 2 * half * (i + 1)]
                out_ref[...] = acc_refs[i][...] + here if acc_refs else here

        @pl.when(pl.program_id(0) > 0)
        def _():
            for i, out_ref in enumerate(outs):
                out_ref[...] += y[2 * half * i : 2 * half * (i + 1)]

    rows = pl.BlockSpec((half, piece), lambda k: (0, which * steps + k))
    full = pl.BlockSpec((2 * half, units), lambda k: (0, 0))
    return pl.pallas_call(
        kernel,
        grid=(steps,),
        in_specs=[rows] * (2 * count)
        + [pl.BlockSpec((units, piece), lambda k: (0, which * steps + k))]
        + [full] * len(accs),
        out_specs=[full] * count,
        out_shape=[jax.ShapeDtypeStruct((2 * half, units), F32)] * count,
        cost_estimate=pl.CostEstimate(
            flops=4 * count * steps * half * piece * units,
            bytes_accessed=2 * steps * piece * units,
            transcendentals=0,
        ),
        compiler_params=params(24),
        name="feedfwd_in",
    )(*(x for part in parts for x in part), streamed(weight), *accs)


def down_products(control, upper, lower, groups, down_flat, segment):
    half = upper.shape[0]
    total = 2 * half
    rows = total // groups
    per = groups // 2
    width = down_flat.shape[1]
    reps = 1
    while (reps * width) % 128:
        reps *= 2
    span = reps * width
    if reps > 1:
        pos = lax.rem(lax.axis_index("mlp"), reps)
        down_flat = jnp.concatenate(
            [jnp.where(pos == i, down_flat, jnp.zeros_like(down_flat)) for i in range(reps)], axis=1
        )
    reqs = REQS
    rank = down_flat.shape[0] // reqs

    def kernel(control_ref, a_ref, b_ref, down_ref, segment_ref, out_ref, x_scratch):
        for i in range(groups):
            start = pl.multiple_of(control_ref[ORDER + i] * rows, rows)
            x = (a_ref if i < per else b_ref)[(i % per) * rows : (i % per + 1) * rows, :]
            x_scratch[pl.ds(start, rows), :] = x

        every_rank = lax.dot_general(
            down_ref[...], x_scratch[...], (((1,), (1,)), ((), ())), preferred_element_type=F32
        ).reshape(reqs, rank, total)
        chosen = lax.broadcasted_iota(jnp.int32, (reqs, total), 0) == segment_ref[...]
        out_ref[...] = jnp.sum(jnp.where(chosen[:, None, :], every_rank, 0.0), axis=0)

    own = pl.BlockSpec((half, span), lambda k, c: (0, c[SPAN]))
    return pl.pallas_call(
        kernel,
        grid_spec=pltpu.PrefetchScalarGridSpec(
            num_scalar_prefetch=1,
            grid=(1,),
            in_specs=[own, own]
            + [pl.BlockSpec(x.shape, lambda k, c: (0, 0)) for x in (down_flat, segment)],
            out_specs=pl.BlockSpec((rank, total), lambda k, c: (0, 0)),
            scratch_shapes=[pltpu.VMEM((total, span), BF16)],
        ),
        out_shape=jax.ShapeDtypeStruct((rank, total), F32),
        cost_estimate=SMALL,
        compiler_params=params(16),
        name="down_products",
    )(control, upper, lower, down_flat, segment)


def feedfwd_out_first(control, accs, lowrank, segments, up_flat, weight, width, tile, groups):
    count, units = accs[0].shape
    parts = len(accs)
    total = parts * count
    reqs, rank = REQS, lowrank.shape[0]
    rows = count // groups

    def kernel(control_ref, *refs):
        acc_refs, segment_refs = (refs[i * parts : (i + 1) * parts] for i in range(2))
        low_ref, up_ref, w_ref, act_ref, kept_ref, sent_ref, up_scratch = refs[2 * parts :]

        @pl.when(pl.program_id(0) == 0)
        def _():
            spreads = []
            for part, segment_ref in enumerate(segment_refs):
                low = low_ref[:, part * count : (part + 1) * count].astype(BF16).astype(F32)
                chosen = lax.broadcasted_iota(jnp.int32, (reqs, count), 0) == segment_ref[...]
                spread = jnp.where(chosen[:, None, :], low[None, :, :], 0.0)
                spreads.append(spread.reshape(reqs * rank, count).astype(BF16))
            up_scratch[...] = lax.dot_general(
                jnp.concatenate(spreads, axis=1),
                up_ref[...],
                (((0,), (0,)), ((), ())),
                preferred_element_type=F32,
            )
            for i in range(groups):
                for part, acc_ref in enumerate(acc_refs):
                    start = pl.multiple_of(part * count + control_ref[ORDER + i] * rows, rows)
                    preact = acc_ref[i * rows : (i + 1) * rows, :] + up_scratch[pl.ds(start, rows), :]
                    here = (i * parts + part) * rows
                    act_ref[here : here + rows, :] = jax.nn.gelu(preact, approximate=True).astype(BF16)

        y = jnp.dot(act_ref[...], w_ref[...], preferred_element_type=F32).astype(BF16)
        kept_ref[...] = y[: total // 2]
        sent_ref[...] = y[total // 2 :]

    half = jax.ShapeDtypeStruct((total // 2, width), BF16)

    def whole(*shape):
        return pl.BlockSpec(shape, lambda j, c: (0,) * len(shape))

    return pl.pallas_call(
        kernel,
        grid_spec=pltpu.PrefetchScalarGridSpec(
            num_scalar_prefetch=1,
            grid=(width // tile,),
            in_specs=[whole(count, units)] * parts
            + [whole(1, count)] * parts
            + [whole(rank, total), whole(reqs * rank, units), pl.BlockSpec((units, tile), lambda j, c: (0, j))],
            out_specs=[whole(total, units)]
            + [pl.BlockSpec((total // 2, tile), lambda j, c: (0, j))] * 2,
            scratch_shapes=[pltpu.VMEM((total, units), F32)],
        ),
        out_shape=[jax.ShapeDtypeStruct((total, units), BF16), half, half],
        cost_estimate=SMALL,
        compiler_params=params(),
        name="feedfwd_out_first",
    )(control, *accs, *segments, lowrank, up_flat, weight)


def pick(held_at, *banks):
    reqs = held_at.shape[0]
    slots, rank = banks[0][0].shape[:2]
    count = len(banks[0])

    def kernel(at_ref, *refs):
        parts = [refs[i * count : (i + 1) * count] for i in range(len(banks))]
        outs = refs[len(banks) * count : -1]
        sems = refs[-1]

        def fetch(i, part, r):
            to = outs[i].at[r * rank : (r + 1) * rank, :]
            return pltpu.make_async_copy(part.at[lax.rem(at_ref[r], slots)], to, sems.at[i, r])

        for r in range(reqs):
            for p in range(count):

                @pl.when(at_ref[r] // slots == p)
                def _():
                    for i in range(len(banks)):
                        fetch(i, parts[i][p], r).start()

        for r in range(reqs):
            for i in range(len(banks)):
                fetch(i, parts[i][0], r).wait()

    return pl.pallas_call(
        kernel,
        grid_spec=pltpu.PrefetchScalarGridSpec(
            num_scalar_prefetch=1,
            grid=(1,),
            in_specs=[pl.BlockSpec(memory_space=pl.ANY)] * (len(banks) * count),
            out_specs=[pl.BlockSpec(memory_space=pl.ANY)] * len(banks),
            scratch_shapes=[pltpu.SemaphoreType.DMA((len(banks), reqs))],
        ),
        out_shape=[jax.ShapeDtypeStruct((reqs * rank, b[0].shape[2]), BF16) for b in banks],
        cost_estimate=SIDE,
        compiler_params=params(16),
        name="pick",
    )(held_at, *(part for bank in banks for part in bank))


def join(arrays, groups):
    rows, width = arrays[0].shape
    depth = width // groups

    per = groups
    steps = groups // per

    def kernel(*refs):
        out_ref = refs[-1]
        for i, ref in enumerate(refs[:-1]):
            for g in range(per):
                out_ref[g, :, i * depth : (i + 1) * depth] = ref[:, g * depth : (g + 1) * depth]

    return pl.pallas_call(
        kernel,
        grid=(steps,),
        in_specs=[pl.BlockSpec((rows, per * depth), lambda g: (0, g))] * len(arrays),
        out_specs=pl.BlockSpec((per, rows, len(arrays) * depth), lambda g: (g, 0, 0)),
        out_shape=jax.ShapeDtypeStruct((groups, rows, len(arrays) * depth), BF16),
        cost_estimate=SMALL,
        compiler_params=params(60),
        name="join",
    )(*arrays)


def attend(control, joined, segment, count, weight):
    total = joined.shape[0]
    depth = joined.shape[1] // 3
    rows = total // count
    first = rows // 2
    width = weight.shape[1]
    tile = width // 4

    def kernel(control_ref, joined_ref, col_ref, row_ref, w_ref, att_ref, kept_ref, sent_ref, x_scratch):
        @pl.when(pl.program_id(0) == 0)
        def _():
            across = lax.broadcasted_iota(jnp.int32, (total, total), 1)
            down = lax.broadcasted_iota(jnp.int32, (total, total), 0)
            allowed = (col_ref[...] == row_ref[...]) & (across <= down)
            for head in range(depth // HS):
                q, k, v = (
                    joined_ref[:, i * depth + head * HS : i * depth + (head + 1) * HS] for i in range(3)
                )
                scores = lax.dot_general(
                    q, k, (((1,), (1,)), ((), ())), preferred_element_type=F32
                ) * (HS ** (-0.5))
                masked = jnp.where(allowed, scores, -1e30)
                exponent = jnp.exp(masked - jnp.max(masked, axis=1, keepdims=True))
                weights = (exponent / jnp.sum(exponent, axis=1, keepdims=True)).astype(BF16)
                mixed = jnp.dot(weights, v, preferred_element_type=F32).astype(BF16)
                att_ref[:, :, head * HS : (head + 1) * HS] = mixed.reshape(count, rows, HS)
            for i in range(count):
                x_scratch[i * first : (i + 1) * first, :] = att_ref[control_ref[ORDER + i], :first, :]

        y = jnp.dot(x_scratch[...], w_ref[...], preferred_element_type=F32).astype(BF16)
        kept_ref[...] = y[: total // 4]
        sent_ref[...] = y[total // 4 :]

    half = jax.ShapeDtypeStruct((total // 4, width), BF16)
    return pl.pallas_call(
        kernel,
        grid_spec=pltpu.PrefetchScalarGridSpec(
            num_scalar_prefetch=1,
            grid=(width // tile,),
            in_specs=[
                pl.BlockSpec((total, 3 * depth), lambda j, o: (0, 0)),
                pl.BlockSpec((total, 1), lambda j, o: (0, 0)),
                pl.BlockSpec((1, total), lambda j, o: (0, 0)),
                pl.BlockSpec((depth, tile), lambda j, o: (0, j)),
            ],
            out_specs=[pl.BlockSpec((count, rows, depth), lambda j, o: (0, 0, 0))]
            + [pl.BlockSpec((total // 4, tile), lambda j, o: (0, j))] * 2,
            scratch_shapes=[pltpu.VMEM((total // 2, depth), BF16)],
        ),
        out_shape=[jax.ShapeDtypeStruct((count, rows, depth), BF16), half, half],
        cost_estimate=SMALL,
        compiler_params=params(48),
        name="attend",
    )(control, joined, segment.reshape(total, 1), segment.reshape(1, total), weight)


def write_pages(joined, lookup, key_cache, value_cache):
    pages, page, depth = key_cache.shape
    blocks = lookup.shape[0]
    hits = lookup[None, :] == jnp.arange(pages, dtype=jnp.int32)[:, None]
    source = jnp.sum(jnp.where(hits, jnp.arange(1, blocks + 1, dtype=jnp.int32)[None, :], 0), axis=1) - 1

    def kernel(source_ref, k_ref, v_ref, key_cache_ref, value_cache_ref, key_ref, value_ref):
        fresh = source_ref[pl.program_id(0)] >= 0

        @pl.when(fresh)
        def _():
            key_ref[0] = k_ref[...]
            value_ref[0] = v_ref[...]

        @pl.when(jnp.logical_not(fresh))
        def _():
            key_ref[...] = key_cache_ref[...]
            value_ref[...] = value_cache_ref[...]

    def block(part):
        return pl.BlockSpec((page, depth), lambda p, source: (jnp.maximum(source[p], 0), part))

    paged = pl.BlockSpec((1, page, depth), lambda p, source: (p, 0, 0))
    return pl.pallas_call(
        kernel,
        grid_spec=pltpu.PrefetchScalarGridSpec(
            num_scalar_prefetch=1,
            grid=(pages,),
            in_specs=[block(1), block(2), paged, paged],
            out_specs=[paged, paged],
        ),
        out_shape=[jax.ShapeDtypeStruct(key_cache.shape, BF16)] * 2,
        cost_estimate=SIDE,
        compiler_params=params(16),
        name="write_pages",
    )(source, joined, joined, key_cache, value_cache)


def shards(
    queries,
    keys,
    values,
    block_hidden_input,
    attention_out_weight,
    feedfwd_in_weight,
    feedfwd_out_weight,
    norm_gain_vector,
    norm_bias_vector,
    adapter_down_factors,
    adapter_up_factors,
    paged_key_cache,
    paged_value_cache,
    request_prompt_length,
    group_page_lookup,
    adapter_per_request,
    adapter_bank_slot,
):
    tok_rows, width = block_hidden_input.shape
    groups = lax.axis_size("mlp")
    group_rows = tok_rows * groups
    head_cols = attention_out_weight.shape[0]
    me = lax.axis_index("mlp")
    bits = [1 << i for i in range(groups.bit_length() - 1)]
    minor = len(bits) - 2
    orders = bits, bits[minor : minor + 1] + bits[:minor] + bits[minor + 1 :]
    steps = list(zip(*orders))
    width_dev = width // groups
    span = width_dev
    while span % 128:
        span *= 2
    first_core = lax.rem(lax.axis_index("req"), 2) == 0
    offsets = [jnp.asarray(block_offsets(masks), jnp.int32) for masks in orders]
    control = jnp.concatenate(
        [jnp.reshape(me * width_dev // span, (1,)), jnp.where(first_core, *offsets) ^ me]
    ).astype(jnp.int32)

    req_masks = [1 << i for i in range(lax.axis_size("req").bit_length() - 1)]
    banks = jnp.swapaxes(adapter_down_factors, 1, 2), adapter_up_factors
    banks = [[x, exchange(x, "req", req_masks[-1])] for x in banks]
    slots = adapter_down_factors.shape[0]
    adapter_ids = adapter_per_request[0]
    matched = (
        adapter_ids[:, None] == jnp.arange(adapter_bank_slot.shape[0], dtype=jnp.int32)[None, :]
    )
    wanted = jnp.sum(jnp.where(matched, adapter_bank_slot[None, :], 0), axis=1)
    part_owner = jnp.asarray(block_offsets(req_masks), jnp.int32) ^ lax.axis_index("req")
    held_slot = (
        part_owner[:, None] * slots + jnp.arange(slots, dtype=jnp.int32)[None, :]
    ).reshape(-1)
    hit = wanted[:, None] == held_slot[None, :]
    held_at = jnp.sum(jnp.where(hit, jnp.arange(hit.shape[1], dtype=jnp.int32)[None, :], 0), axis=1)

    joined = lax.all_to_all(
        join((queries, keys, values), groups), "mlp", split_axis=0, concat_axis=0, tiled=True
    ).reshape(group_rows, 3 * head_cols)

    request_ends = jnp.cumsum(request_prompt_length[0])
    positions = jnp.arange(group_rows, dtype=jnp.int32)
    segment = jnp.sum((positions[:, None] >= request_ends[None, :]).astype(jnp.int32), axis=1)
    joined, segment, control, held_at = tied(joined, segment, control, held_at)
    attended, *partial_a = attend(control, joined, segment, groups, attention_out_weight)
    partial_b = out_projection(control, attended, 1, attention_out_weight)
    kept_a, sent_a = reduce_step(*partial_a, steps[0])
    sent_a = after(sent_a, partial_b)

    sent_a, joined, banks = tied(sent_a, joined, banks)
    for mask in req_masks[-2::-1]:
        banks = [parts + [exchange(part, "req", mask) for part in parts] for parts in banks]
    pages_out = write_pages(joined, group_page_lookup[0], paged_key_cache, paged_value_cache)
    factors = pick(held_at, *banks)

    vectors = norm_gain_vector, norm_bias_vector
    sum_a = reduce_rows(kept_a, sent_a, steps[1:])
    partial_b = reduce_step(*partial_b, steps[0])
    sum_a = after(sum_a, partial_b)
    residual_a, rows_a = norm(block_hidden_input, 0, sum_a, *vectors)
    for masks in steps[1:-1]:
        partial_b = reduce_step(*partial_b, masks)
    rows_a = grow(rows_a, steps[-1], partial_b)
    sum_b, (key_pages_out, value_pages_out), (down_flat, up_flat), _ = tied(
        reduce_rows(*partial_b, steps[-1:]), pages_out, factors, rows_a
    )
    residual_b, rows_b = norm(block_hidden_input, 1, sum_b, *vectors)
    ahead = steps[-2::-1]
    for masks, masks_ahead in zip(steps[:0:-1], ahead):
        if masks_ahead is steps[0]:
            rows_a = rows_a, swap(rows_a, masks_ahead)
            rows_b = grow(rows_b, masks, rows_a[1])
        else:
            rows_a = grow(rows_a, masks_ahead)
            rows_b = grow(rows_b, masks, rows_a)
    rows_b = rows_b, swap(rows_b, steps[0])

    part_rows = tok_rows // 2
    segments = [
        segment.reshape(groups, 2, part_rows)[:, part].reshape(1, groups * part_rows)
        for part in range(2)
    ]
    win = feedfwd_in_weight.T
    low_a = down_products(control, *rows_a, groups, down_flat, segments[0])
    acc_a = feedfwd_in([rows_a], win, 0)
    rows_b, low_a, acc_a = tied(rows_b, low_a, acc_a)
    low_b = down_products(control, *rows_b, groups, down_flat, segments[1])
    lowrank = jnp.concatenate([low_a, low_b], axis=1)
    acc_b = feedfwd_in([rows_b], win, 0)
    for mask in bits[:minor]:
        lowrank = lowrank + exchange(lowrank, "mlp", mask)
    lowrank, acc_b = tied(lowrank, acc_b)
    lowrank = lowrank + sum(
        exchange(lowrank, "mlp", k << minor) for k in range(1, groups >> minor)
    )
    acc = feedfwd_in([rows_a, rows_b], win, 1, acc_a + acc_b)

    wide = width // 2
    tile = wide // 2
    activated, *partial_a = feedfwd_out_first(
        control, acc, lowrank, segments, up_flat, feedfwd_out_weight, wide, tile, groups
    )
    partial_b = feedfwd_out(activated, feedfwd_out_weight, wide, width - wide, tile)
    partial_a = reduce_step(*partial_a, steps[0])
    partial_b = reduce_step(*after(partial_b, partial_a), steps[0])
    for masks in steps[1:-1]:
        partial_a = reduce_step(*partial_a, masks)
        partial_b = reduce_step(*after(partial_b, partial_a), masks)
    sums = (
        (partial_a[0], swap(partial_a[1], steps[-1])),
        (partial_b[0], swap(partial_b[1], steps[-1])),
    )
    block_out = (
        jnp.concatenate([residual_a, residual_b], axis=0)
        + jnp.concatenate([a.astype(F32) + b.astype(F32) for a, b in sums], axis=1)
    ).astype(BF16)
    return (block_out, key_pages_out, value_pages_out)


def solution(mesh):
    in_specs = (
        P(("req", "mlp"), None),
        P(("req", "mlp"), None),
        P(("req", "mlp"), None),
        P(("req", "mlp"), None),
        P("mlp", None),
        P(None, "mlp"),
        P("mlp", None),
        P(),
        P(),
        P("req", "mlp", None),
        P("req", None, "mlp"),
        P("req", None, "mlp"),
        P("req", None, "mlp"),
        P("req", None),
        P("req", None),
        P("req", None),
        P(),
    )
    out_specs = (P(("req", "mlp"), None), P("req", None, "mlp"), P("req", None, "mlp"))
    return jax.shard_map(shards, mesh=mesh, in_specs=in_specs, out_specs=out_specs, check_vma=False)
```
